256 devices in a mesh: rep: 16 (over z, core), fsdp: 16 (over y, x).
Axes of the slice: x: 4, y: 4, z: 8, core: 2. Of those that a mesh axis runs over, the one named last changes fastest.
Arguments:
- gradients: bfloat16 [16, 4, 1024, 8192], P('rep', None, None, 'fsdp'), may hold values from -12 to 12
- old_left: float32 [64, 1024, 1024], P('fsdp', 'rep'), may hold values from -6 to 6
- old_right: float32 [64, 1024, 1024], P('fsdp', 'rep'), may hold values from -6 to 6
- left_root: float32 [64, 1024, 1024], P('fsdp', 'rep'), may hold values from -20 to 20, as said below
- right_root: float32 [64, 1024, 1024], P('fsdp', 'rep'), may hold values from -20 to 20, as said below
- owner_plan: int32 [4, 8], replicated, may hold values from 0 to 15, as said below
Outputs:
- new_left: float32 [64, 1024, 1024], P('fsdp', 'rep')
- new_right: float32 [64, 1024, 1024], P('fsdp', 'rep')
- direction: bfloat16 [4, 1024, 8192], P(None, 'rep', 'fsdp')
The draws below stay inside these ranges and needn't reach their ends.
Inputs may be any that keep to these rules, and one draw needn't show every extreme that they name: `owner_plan`: no fsdp index owns more than 4 blocks, and some index owns exactly 4. `left_root`: every one of the 64 blocks is symmetric. `right_root`: every one of the 64 blocks is symmetric.
All inputs are finite; a program needn't handle non-finite values.
Results may differ from the reference program's by a relative error of at most 0.025.
Values may be sent and summed in bfloat16 or wider, within the bound.
A program may use at most 128 MiB of HBM per device.

```python
import jax
import jax.numpy as jnp
from jax import lax

D = 8192
KV = 1024
BLK = 1024
LAYERS = 4
NBR = 8
NB = 32
SLOTS = 4
N_REP = 16
N_FSDP = 16


def symmetric_root(key, spread, low_diag, high_diag):
    first_key, second_key = jax.random.split(key, 2)
    block_total = N_FSDP * SLOTS
    noise = jax.random.normal(first_key, (block_total, BLK, BLK), jnp.float32)
    paired = (noise + jnp.swapaxes(noise, 1, 2)) * (0.5 * spread)
    diagonal = jax.random.uniform(second_key, (block_total, BLK), jnp.float32, low_diag, high_diag)
    eye_matrix = jnp.eye(BLK, dtype=jnp.float32)
    matrix = paired + eye_matrix[None] * diagonal[:, :, None]
    return matrix


def draw_left_root(key, part):
    key = jax.random.fold_in(key, 21)
    return symmetric_root(key, 0.02, 0.5, 1.5)


def draw_right_root(key, part):
    key = jax.random.fold_in(key, 37)
    return symmetric_root(key, 0.02, 0.5, 1.5)


def draw_owner_plan(key, part):
    key = jax.random.fold_in(key, 53)
    first_key, second_key, third_key = jax.random.split(key, 3)
    heavy_owner = jax.random.randint(first_key, (), 0, N_FSDP)
    others = jax.random.permutation(second_key, (N_FSDP - 1) * SLOTS)[:NB - SLOTS] // SLOTS
    devices = (heavy_owner + 1 + others) % N_FSDP
    listed = jnp.concatenate([jnp.full((SLOTS,), heavy_owner, jnp.int32), devices.astype(jnp.int32)])
    shuffle = jax.random.permutation(third_key, NB)
    return listed[shuffle].reshape(LAYERS, NBR).astype(jnp.int32)


def level_of(key, dims, pieces, low, largest):
    def one(axis_at, blocks):
        draws = jax.random.uniform(jax.random.fold_in(jax.random.fold_in(key, 6), axis_at), (blocks,), jnp.float32, low / len(pieces), largest / len(pieces))
        return jnp.repeat(jnp.exp(draws), dims[axis_at] // blocks).reshape((-1,) + (1,) * (len(dims) - axis_at - 1))

    gain = one(*pieces[0])
    for cut in pieces[1:]:
        gain = gain * one(*cut)
    return gain


def centred(stream_key, extent, scale, limit, pieces=(), kind=jnp.bfloat16):
    result = scale * jax.random.normal(stream_key, extent, jnp.float32)
    if pieces:
        result = result * level_of(stream_key, extent, pieces, -0.22, 0.18)
    return jnp.clip(result, -limit, limit).astype(kind)


def setup_inputs(seed: int = 0) -> dict:
    key_list = jax.random.split(jax.random.key(seed), 7)
    gradients = centred(key_list[0], (N_REP, LAYERS, KV, D), 2.0, 12.0, ((0, 16), (3, 16)))
    old_left = centred(key_list[1], (N_FSDP * SLOTS, BLK, BLK), 1.0, 6.0, ((0, 16), (1, 16)), jnp.float32)
    old_right = centred(key_list[2], (N_FSDP * SLOTS, BLK, BLK), 1.0, 6.0, ((0, 16), (1, 16)), jnp.float32)
    left_root = draw_left_root(jax.random.fold_in(key_list[6], 71), 0)
    right_root = draw_right_root(jax.random.fold_in(key_list[6], 71), 0)
    owner_plan = draw_owner_plan(jax.random.fold_in(key_list[6], 71), 0)
    return {"gradients": gradients, "old_left": old_left, "old_right": old_right, "left_root": left_root, "right_root": right_root, "owner_plan": owner_plan}


gram_decay = 0.95


def ownership(owner_plan):
    owners = owner_plan.reshape(-1)
    positions = jnp.arange(owners.shape[0], dtype=jnp.int32)
    earlier = (owners[:, None] == owners[None, :]) & (positions[None, :] < positions[:, None])
    return owners, jnp.sum(earlier.astype(jnp.int32), axis=1).astype(jnp.int32)


def reference(gradients, old_left, old_right, left_root, right_root, owner_plan):
    owners, slot_of = ownership(owner_plan)
    slot_index = (owners * SLOTS + slot_of).astype(jnp.int32)
    summed = jnp.sum(gradients.astype(jnp.float32), axis=0)
    reduced = (summed / N_REP).astype(jnp.bfloat16)
    grad_blocks = reduced.reshape(LAYERS, KV, NBR, BLK).transpose(0, 2, 1, 3).reshape(NB, KV, BLK)

    def one_block(inputs):
        grad_block, where_slot = inputs
        gram_left = jnp.dot(grad_block, grad_block.T, preferred_element_type=jnp.float32)
        gram_right = jnp.dot(grad_block.T, grad_block, preferred_element_type=jnp.float32)
        right_block = right_root[where_slot]
        left_block = left_root[where_slot]
        right_product = jnp.dot(grad_block.astype(jnp.float32), right_block,
                                precision=lax.Precision.HIGHEST).astype(jnp.bfloat16)
        block_direction = jnp.dot(left_block, right_product.astype(jnp.float32),
                                  precision=lax.Precision.HIGHEST).astype(jnp.bfloat16)
        return gram_left, gram_right, block_direction

    grams_left, grams_right, block_dirs = lax.map(one_block, (grad_blocks, slot_index))
    new_left = gram_decay * old_left
    new_left = new_left.at[slot_index].set(gram_decay * old_left[slot_index] + (1.0 - gram_decay) * grams_left)
    new_right = gram_decay * old_right
    new_right = new_right.at[slot_index].set(gram_decay * old_right[slot_index] + (1.0 - gram_decay) * grams_right)
    direction = block_dirs.reshape(LAYERS, NBR, KV, BLK).transpose(0, 2, 1, 3).reshape(LAYERS, KV, D)
    return new_left, new_right, direction
```

```python
import functools

import jax
import jax.numpy as jnp
from jax import lax
from jax.experimental import pallas as pl
from jax.experimental.pallas import tpu as pltpu
from jax.sharding import PartitionSpec as P

gram_decay = 0.95
MESH = pl.DeviceIdType.MESH
F32 = jnp.float32
BF16 = jnp.bfloat16


class Dims:
    def __init__(self, rep, fsdp, layers, rows, home, slots):
        self.NR, self.NF, self.NZ = rep, fsdp, rep // 2
        self.FX = 4 if fsdp == 16 else 2
        self.FY = fsdp // self.FX
        self.H = self.NZ // 2
        self.STEPS = 2 * self.H - 1
        self.BLK = rows
        self.SR = rows // rep
        self.HC = home
        self.CH = home // 2
        self.SLOTS = slots
        self.CG = 4 if fsdp == 16 else 2
        self.RG = fsdp // self.CG
        self.PR, self.PC = self.SR // self.RG, rows // self.CG


def kernel(
    d,
    grad,
    old_left,
    old_right,
    left_root,
    right_root,
    owner_plan,
    new_left,
    new_right,
    dir_out,
    plan,
    tab_v,
    tab,
    own,
    sib,
    rs_send,
    rs_recv,
    total,
    roots,
    olds,
    send_a,
    recv_a,
    swap_b,
    send_b,
    recv_b,
    Lp,
    Rs,
    Gb,
    Rb,
    g_s,
    left_sum,
    T_s,
    D_s,
    swap_c,
    send_c,
    recv_c0,
    recv_c1,
    send_d,
    recv_d,
    Db,
    own_sem,
    root_sem,
    old_sem,
    plan_sem,
    tab_sem,
    sib_ss,
    sib_rs,
    rs_ss,
    rs_rs,
    aa_ss,
    aa_rs,
    sw_ss,
    sw_rs,
    ex_ss,
    ex_rs,
    ag_ss,
    ag_rs,
):
    NZ, H, NF, FX, FY, STEPS = d.NZ, d.H, d.NF, d.FX, d.FY, d.STEPS
    r, f = lax.axis_index("rep"), lax.axis_index("fsdp")
    z, c = lax.div(r, 2), lax.rem(r, 2)
    y, x = lax.div(f, FX), lax.rem(f, FX)
    q = lax.rem(f, 2)
    up, down = lax.rem(z + 1, NZ) * 2 + c, lax.rem(z + NZ - 1, NZ) * 2 + c
    sibling = z * 2 + 1 - c
    partner = f + 1 - 2 * q

    around = [lax.rem(z + k, NZ) for k in range(NZ)]

    def zat(dist):
        return around[dist % NZ]

    def remote(src, dst, ss, rs, **where):
        return pltpu.make_async_remote_copy(
            src_ref=src, dst_ref=dst, send_sem=ss, recv_sem=rs, device_id=where, device_id_type=MESH
        )

    order = [H]
    for k in range(H - 1, 0, -1):
        order += [k, NZ - k]
    order += [0]

    def own_copy(k):
        return pltpu.make_async_copy(grad.at[:, c, zat(k)], own.at[k], own_sem.at[k])

    def root_copy(m):
        return pltpu.make_async_copy((left_root, right_root)[m], roots.at[m], root_sem.at[m])

    def old_copy(m, s):
        return pltpu.make_async_copy((old_left, old_right)[m].at[s], olds.at[m, s], old_sem.at[m, s])

    plan_copy = pltpu.make_async_copy(owner_plan, plan, plan_sem)
    tab_copy = pltpu.make_async_copy(tab_v, tab, tab_sem)

    barrier = pltpu.get_barrier_semaphore()

    ys = [lax.rem(y + k, FY) * FX for k in range(FY)]
    xs = [lax.rem(x + k, FX) for k in range(FX)]
    peers = [ys[i // FX] + xs[i % FX] for i in range(1, NF)]
    for where in ({"rep": sibling}, {"rep": up}, {"rep": down}, {"rep": sibling, "fsdp": partner}):
        pl.semaphore_signal(barrier, inc=1, device_id=where, device_id_type=MESH)
    for peer in peers:
        pl.semaphore_signal(barrier, inc=1, device_id={"fsdp": peer}, device_id_type=MESH)
    for k in order:
        own_copy(k).start()
    for m in range(2):
        root_copy(m).start()
    plan_copy.start()
    pl.semaphore_wait(barrier, NF - 1 + 4)

    def cut(value, piece):
        rg, cg = piece // d.CG, piece % d.CG
        return value[rg * d.PR : (rg + 1) * d.PR, cg * d.PC : (cg + 1) * d.PC]

    def cast_root(m):
        root_copy(m).wait()

        def go(s, carry):
            value = roots[m, s].astype(BF16)
            for piece in range(NF):
                send_a[piece * d.SLOTS + s, m] = cut(value, piece)
            return carry

        lax.fori_loop(0, d.SLOTS, go, 0)

    layers, columns = plan.shape
    blocks = layers * columns

    def tables():
        plan_copy.wait()
        owner = [plan[b // columns, b % columns] for b in range(blocks)]
        row = lax.broadcasted_iota(jnp.int32, (blocks, 128), 0)
        lane = lax.broadcasted_iota(jnp.int32, (blocks, 128), 1)
        owners = jnp.zeros((blocks, 128), jnp.int32)
        for b in range(blocks):
            owners = jnp.where(row == b, owner[b], owners)
        index = owners * d.SLOTS
        for b in range(blocks - 1):
            index = index + jnp.where((row > b) & (owners == owner[b]), 1, 0)
        places = jnp.zeros((blocks, 128), jnp.int32)
        for b in range(blocks):
            l, j = b // columns, b % columns
            places = jnp.where(row == b, (2 * j + l // 2) * 2 + l % 2, places)
        held = jnp.max(jnp.where(index == lane, places, -1), axis=0, keepdims=True)
        tab_v[0:blocks] = index
        tab_v[blocks : blocks + 8] = jnp.broadcast_to(held, (8, 128))
        tab_copy.start()

    def sib_copy(i, k):
        return remote(
            grad.at[:, 1 - c, zat(k), :, pl.ds(i * d.CH, d.CH)],
            sib.at[i, k],
            sib_ss.at[i],
            sib_rs.at[i, k],
            rep=sibling,
        )

    def rs_items(stream):
        items = [(H, stream)]
        for k in range(H - 1, 0, -1):
            items += [(k, 1 - stream), (k, stream)]
        return items

    def rs_slot(stream, dist, half):
        items = rs_items(stream)
        return items.index((dist, half)) if (dist, half) in items else None

    def rs_copy(i, stream, k):
        return remote(
            rs_send.at[i, stream, k],
            rs_recv.at[i, stream, k],
            rs_ss.at[i, stream],
            rs_rs.at[i, stream, k],
            rep=(up, down)[stream],
        )

    ready = set()

    def base(i, k, half):
        if k not in ready:
            own_copy(k).wait()
            ready.add(k)
        if (i, k) not in ready:
            sib_copy(i, k).wait_recv()
            ready.add((i, k))
        mine = own[k, half, :, i * d.CH : (i + 1) * d.CH]
        return mine.astype(F32) + sib[i, k, half].astype(F32)

    def rs_step(i, *steps):
        for k in steps:
            if k >= STEPS:
                continue
            for stream in range(2):
                dist, half = rs_items(stream)[k]
                value = base(i, dist if stream == 0 else NZ - dist, half)
                before = rs_slot(stream, dist + 1, half)
                if before is not None:
                    rs_copy(i, stream, before).wait_recv()
                    value = value + rs_recv[i, stream, before].astype(F32)
                rs_send[i, stream, k] = value.astype(BF16)
                rs_copy(i, stream, k).start()

    def ex_g(i):
        return remote(total.at[i, 1 - q], Gb.at[i, z, q], ex_ss.at[i], ex_rs.at[i], fsdp=partner)

    def rs_last(i):
        for half in range(2):
            value = base(i, 0, half)
            for stream in range(2):
                k = rs_slot(stream, 1, half)
                rs_copy(i, stream, k).wait_recv()
                value = value + rs_recv[i, stream, k].astype(F32)
            total[i, half] = (value / d.NR).astype(BF16)
        ex_g(i).start()
        Gb[i, z, q] = total[i, q]

    def aa_start(phase, send, recv):
        size = recv.shape[0] // NF
        part = recv.at[pl.ds(f * size, size)]
        sems = aa_ss.at[phase], aa_rs.at[phase]
        for to in peers:
            remote(send.at[pl.ds(to * size, size)], part, *sems, fsdp=to).start()
        recv[pl.ds(f * size, size)] = send[pl.ds(f * size, size)]

    def aa_all(phase, send, recv):
        most = pl.ds(0, recv.shape[0] // NF * (NF - 1))
        return remote(send.at[most], recv.at[most], aa_ss.at[phase], aa_rs.at[phase], fsdp=partner)

    def aa_wait(phase, send, recv):
        aa_all(phase, send, recv).wait_recv()

    def aa_done(phase, send, recv):
        aa_all(phase, send, recv).wait_send()

    def ag_items(stream):
        items = []
        for k in range(H - 1):
            items += [(k, stream), (k, 1 - stream)]
        return items + [(H - 1, stream)]

    bufs = (Gb.at[0], Gb.at[1], Rb)

    def ag_copy(a, stream, k, ahead):
        dist, half = ag_items(stream)[k]
        part = bufs[a].at[zat(-dist - ahead if stream == 0 else dist + ahead), half]
        return remote(part, part, ag_ss.at[a], ag_rs.at[a, stream, k], rep=(up, down)[stream])

    def ag_own(a):
        for k in range(2):
            for stream in range(2):
                ag_copy(a, stream, k, 0).start()

    def ag_step(a, *steps):
        for k in steps:
            if k >= STEPS:
                continue
            for stream in range(2):
                ag_copy(a, stream, k, 1).wait_recv()
                if k + 2 < STEPS:
                    ag_copy(a, stream, k + 2, 0).start()

    def ag_done(a):
        part = bufs[a].at[pl.ds(0, STEPS)]
        remote(part, part, ag_ss.at[a], ag_rs.at[a, 0, 0], rep=up).wait_send()

    wide = 2 * d.SR

    swap_roots = remote(swap_b, send_b.at[:, c], sw_ss.at[0], sw_rs.at[0], rep=sibling)

    def pick_roots():
        def go(p, carry):
            for core, to in ((1 - c, 0), (c, 1)):
                where = tab[(lax.rem(p, 2) * 2 + core) * columns + lax.div(p, 2), 0]
                for m in range(2):
                    value = recv_a[where, m]
                    if to == 0:
                        swap_b[p, m] = value
                    else:
                        send_b[p, c, m] = value
            return carry

        lax.fori_loop(0, NF, go, 0)
        swap_roots.start()

    def join_roots():
        for piece in range(NF):
            rg, cg = piece // d.CG, piece % d.CG
            cols = pl.ds(cg * d.PC, d.PC)
            for core in range(2):
                Lp[pl.ds(core * d.SR + rg * d.PR, d.PR), cols] = recv_b[piece, core, 0]
                Rs[pl.ds(core * d.SR + rg * d.PR, d.PR), cols] = recv_b[piece, core, 1]
        for dist in range(H + 1):
            at = pl.multiple_of(zat(dist) * wide, wide)
            for core in range(2):
                Rb[z, core, :, dist * wide : (dist + 1) * wide] = Rs[
                    core * d.SR : (core + 1) * d.SR, pl.ds(at, wide)
                ]

    def block(i, half):
        return Gb[i, :, half].reshape(d.BLK, d.CH)

    recv_c = (recv_c0, recv_c1)

    def swap_gram(m):
        return remote(swap_c.at[m], send_c.at[m, :, c], sw_ss.at[1 + m], sw_rs.at[1 + m], rep=sibling)

    def put_gram(m):
        value = g_s[m, 1 - c]
        for piece in range(NF):
            swap_c[m, piece] = cut(value, piece)
        swap_gram(m).start()
        value = g_s[m, c]
        for piece in range(NF):
            send_c[m, piece, c] = cut(value, piece)

    def gram_left(i):
        value = 0.0 if i == 0 else left_sum[...]
        for h in range(2):
            value = value + lax.dot_general(
                Gb[i, z, h], block(i, h), (((1,), (1,)), ((), ())), preferred_element_type=F32
            )
        if i == 0:
            left_sum[...] = value
        else:
            g_s[0] = ((1.0 - gram_decay) * value).astype(BF16).reshape(2, d.SR, d.BLK)
            put_gram(0)

    def gram_right():
        at = z * wide
        half, chain, off = at // d.HC, at % d.HC // d.CH, at % d.CH
        cols = Gb[chain, :, half, :, pl.ds(pl.multiple_of(off, wide), wide)]
        cols = cols.reshape(d.BLK, wide)
        for i in range(2):
            for h in range(2):
                both = lax.dot_general(
                    cols, block(i, h), (((0,), (0,)), ((), ())), preferred_element_type=F32
                )
                both = ((1.0 - gram_decay) * both).astype(BF16)
                first = h * d.HC + i * d.CH
                g_s[1, :, :, first : first + d.CH] = both.reshape(2, d.SR, d.CH)
        put_gram(1)

    def left_times(i):
        for h in range(2):
            first = h * d.HC + i * d.CH
            value = jnp.dot(Lp[...], block(i, h), preferred_element_type=F32).astype(BF16)
            for t in range(d.CH // wide):
                T_s[first // wide + t] = value[:, t * wide : (t + 1) * wide]

    def pick_grams(m):
        def go(o, carry):
            for s in range(d.SLOTS):
                where = jnp.maximum(tab[blocks, o * d.SLOTS + s], 0)
                send_d[m, o * d.SLOTS + s] = recv_c[m][lax.div(where, 2), lax.rem(where, 2)]
            return carry

        lax.fori_loop(0, NF, go, 0)

    def add_grams(m):
        for s in range(d.SLOTS):
            old_copy(m, s).wait()

        def go(s, carry):
            live = tab[blocks, f * d.SLOTS + s] >= 0
            for piece in range(NF):
                rg, cg = piece // d.CG, piece % d.CG
                rows, cols = pl.ds(rg * d.PR, d.PR), pl.ds(cg * d.PC, d.PC)
                added = jnp.where(live, recv_d[m, piece * d.SLOTS + s].astype(F32), 0.0)
                (new_left, new_right)[m][s, rows, cols] = (
                    gram_decay * olds[m, s, rows, cols] + added
                )
            return carry

        lax.fori_loop(0, d.SLOTS, go, 0)

    homes = (
        remote(Db.at[c, 1 - q], dir_out.at[q, c], ex_ss.at[2], ex_rs.at[2], fsdp=partner),
        remote(Db.at[1 - c, q], dir_out.at[q, c], ex_ss.at[3], ex_rs.at[3], rep=sibling),
        remote(
            Db.at[1 - c, 1 - q], dir_out.at[q, c], ex_ss.at[4], ex_rs.at[4], rep=sibling, fsdp=partner
        ),
    )

    def add_slab(dist):
        k = zat(dist)
        root = Rb[k].reshape(wide, (H + 1) * wide)
        direct = jnp.dot(T_s[k], root, preferred_element_type=F32)
        for t in range(H + 1):
            D_s[zat(dist + t)] += direct[:, t * wide : (t + 1) * wide]
        turned = jnp.concatenate([T_s[zat(dist + t)] for t in range(1, H)], axis=1)
        D_s[k] += lax.dot_general(
            turned, root[:, wide : H * wide], (((1,), (1,)), ((), ())), preferred_element_type=F32
        )

    def directions():
        for k in range(NZ):
            value = D_s[k].astype(BF16).reshape(2, d.SR, wide)
            half, at = divmod(k * wide, d.HC)
            Db[:, half, :, at : at + wide] = value
        for copy in homes:
            copy.start()
        dir_out[q, c] = Db[c, q]

    def fetch_old(s):
        for m in range(2):
            old_copy(m, s).start()

    for k in order[:3]:
        sib_copy(0, k).start()
    rs_step(0, 0)
    for k in order[3:]:
        sib_copy(0, k).start()
    rs_step(0, 1)
    for k in order:
        sib_copy(1, k).start()
    rs_step(1, 0)
    cast_root(0)
    rs_step(0, 2)
    rs_step(1, 1)
    cast_root(1)
    aa_start(0, send_a, recv_a)
    rs_step(0, 3)
    rs_step(1, 2)
    tables()
    rs_step(0, 4)
    rs_step(1, 3)
    rs_step(0, 5)
    rs_step(1, 4)
    rs_step(0, 6)
    rs_step(1, 5)
    rs_last(0)
    rs_step(1, 6)
    ex_g(0).wait_recv()
    ag_own(0)
    rs_last(1)
    ag_step(0, 0)
    ex_g(1).wait_recv()
    ag_own(1)
    ag_step(0, 1)
    aa_wait(0, send_a, recv_a)
    tab_copy.wait()
    pick_roots()
    ag_step(0, 2)
    ag_step(1, 0)
    swap_roots.wait_recv()
    aa_start(1, send_b, recv_b)
    ag_step(0, 3)
    ag_step(1, 1)
    fetch_old(0)
    ag_step(0, 4)
    ag_step(1, 2)
    fetch_old(1)
    ag_step(0, 5)
    ag_step(1, 3)
    fetch_old(2)
    ag_step(0, 6)
    gram_left(0)
    ag_step(1, 4)
    fetch_old(3)
    aa_wait(1, send_b, recv_b)
    join_roots()
    ag_own(2)
    ag_step(1, 5, 6)
    gram_left(1)
    gram_right()
    ag_step(2, 0)
    swap_gram(0).wait_recv()
    aa_start(2, send_c.at[0], recv_c0)
    swap_gram(1).wait_recv()
    aa_start(3, send_c.at[1], recv_c1)
    ag_step(2, 1)
    left_times(0)
    aa_wait(2, send_c.at[0], recv_c0)
    pick_grams(0)
    aa_start(4, send_d.at[0], recv_d.at[0])
    ag_step(2, 2)
    aa_wait(3, send_c.at[1], recv_c1)
    pick_grams(1)
    aa_start(5, send_d.at[1], recv_d.at[1])
    ag_step(2, 3)
    left_times(1)
    D_s[...] = jnp.zeros_like(D_s)
    add_slab(0)
    ag_step(2, 4)
    for dist in range(1, min(3, H)):
        add_slab(-dist)
        add_slab(dist)

    for i in range(2):
        remote(sib.at[i], sib.at[i], sib_ss.at[i], sib_rs.at[i, 0], rep=sibling).wait_send()
        for stream in range(2):
            sent = rs_send.at[i, stream]
            remote(sent, sent, rs_ss.at[i, stream], rs_rs.at[i, stream, 0], rep=up).wait_send()
        ex_g(i).wait_send()
        ag_done(i)
    aa_done(0, send_a, recv_a)
    aa_done(1, send_b, recv_b)
    swap_roots.wait_send()
    for m in range(2):
        swap_gram(m).wait_send()
        aa_done(2 + m, send_c.at[m], recv_c[m])

    ag_step(2, 5)
    for dist in range(3, H):
        add_slab(-dist)
        add_slab(dist)
    ag_step(2, 6)
    add_slab(H)
    directions()
    for m in range(2):
        aa_wait(4 + m, send_d.at[m], recv_d.at[m])
        add_grams(m)
    ag_done(2)
    for m in range(2):
        aa_done(4 + m, send_d.at[m], recv_d.at[m])
    for copy in homes:
        copy.wait()


def local(gradients, old_left, old_right, left_root, right_root, owner_plan):
    rep, fsdp = lax.axis_size("rep"), lax.axis_size("fsdp")
    _, layers, rows, home = gradients.shape
    slots = old_left.shape[0]
    d = Dims(rep, fsdp, layers, rows, home, slots)

    S, NZ, NF = d.STEPS, d.NZ, d.NF
    CR = 2 * d.SR
    piece = (d.PR, d.PC)
    vmem = lambda *shape: pltpu.VMEM(shape, BF16)
    wide = lambda *shape: pltpu.VMEM(shape, F32)
    dma = lambda *shape: pltpu.SemaphoreType.DMA(shape)
    whole = pl.BlockSpec(memory_space=pltpu.VMEM)
    away = pl.BlockSpec(memory_space=pl.ANY)
    new_left, new_right, direction = pl.pallas_call(
        functools.partial(kernel, d),
        out_shape=(
            jax.ShapeDtypeStruct(old_left.shape, F32),
            jax.ShapeDtypeStruct(old_right.shape, F32),
            jax.ShapeDtypeStruct((2, 2, d.SR, d.HC), BF16),
        ),
        in_specs=[away] * 6,
        out_specs=(whole,) * 3,
        scratch_shapes=[
            pltpu.SMEM(owner_plan.shape, jnp.int32),
            pltpu.VMEM((owner_plan.size + 8, 128), jnp.int32),
            pltpu.SMEM((owner_plan.size + 8, 128), jnp.int32),
            vmem(NZ, 2, CR, d.HC),
            vmem(2, NZ, 2, CR, d.CH),
            vmem(2, 2, S, CR, d.CH),
            vmem(2, 2, S, CR, d.CH),
            vmem(2, 2, CR, d.CH),
            wide(2, slots, d.SR, d.BLK),
            wide(2, slots, d.SR, d.BLK),
            vmem(NF * slots, 2, *piece),
            vmem(NF * slots, 2, *piece),
            vmem(NF, 2, *piece),
            vmem(NF, 2, 2, *piece),
            vmem(NF, 2, 2, *piece),
            vmem(CR, d.BLK),
            vmem(CR, d.BLK),
            vmem(2, NZ, 2, CR, d.CH),
            vmem(NZ, 2, d.SR, (d.H + 1) * CR),
            vmem(2, 2, d.SR, d.BLK),
            wide(CR, d.BLK),
            vmem(NZ, CR, CR),
            wide(NZ, CR, CR),
            vmem(2, NF, *piece),
            vmem(2, NF, 2, *piece),
            vmem(NF, 2, *piece),
            vmem(NF, 2, *piece),
            vmem(2, NF * slots, *piece),
            vmem(2, NF * slots, *piece),
            vmem(2, 2, d.SR, d.HC),
            dma(NZ),
            dma(2),
            dma(2, slots),
            pltpu.SemaphoreType.DMA,
            pltpu.SemaphoreType.DMA,
            dma(2),
            dma(2, NZ),
            dma(2, 2),
            dma(2, 2, S),
            dma(6),
            dma(6),
            dma(3),
            dma(3),
            dma(5),
            dma(5),
            dma(3),
            dma(3, 2, S),
        ],
        compiler_params=pltpu.CompilerParams(
            collective_id=0, has_side_effects=True, vmem_limit_bytes=51 * 1024 * 1024
        ),
        cost_estimate=pl.CostEstimate(
            flops=2 * 5 * 2 * d.SR * d.BLK * d.BLK,
            bytes_accessed=2 * gradients.size + 24 * left_root.size,
            transcendentals=0,
        ),
    )(
        gradients.reshape(2, 2, NZ, CR, home),
        old_left,
        old_right,
        left_root,
        right_root,
        owner_plan,
    )
    return new_left, new_right, direction.reshape(layers, d.SR, home)


def solution(mesh):
    return jax.shard_map(
        local,
        mesh=mesh,
        in_specs=(
            P("rep", None, None, "fsdp"),
            P("fsdp", "rep", None),
            P("fsdp", "rep", None),
            P("fsdp", "rep", None),
            P("fsdp", "rep", None),
            P(),
        ),
        out_specs=(P("fsdp", "rep", None), P("fsdp", "rep", None), P(None, "rep", "fsdp")),
        check_vma=False,
    )
```

```python
import functools

import jax
import jax.numpy as jnp
from jax import lax
from jax.experimental import pallas as pl
from jax.experimental.pallas import tpu as pltpu
from jax.sharding import PartitionSpec as P

gram_decay = 0.95
MESH = pl.DeviceIdType.MESH
F32 = jnp.float32
BF16 = jnp.bfloat16


class Dims:
    def __init__(self, rep, fsdp, layers, rows, home, slots):
        self.NR, self.NF, self.NZ = rep, fsdp, rep // 2
        self.FX = 4 if fsdp == 16 else 2
        self.FY = fsdp // self.FX
        self.H = self.NZ // 2
        self.STEPS = 2 * self.H - 1
        self.BLK = rows
        self.SR = rows // rep
        self.HC = home
        self.CH = home // 2
        self.SLOTS = slots
        self.CG = 4 if fsdp == 16 else 2
        self.RG = fsdp // self.CG
        self.PR, self.PC = self.SR // self.RG, rows // self.CG


def kernel(
    d,
    grad,
    old_left,
    old_right,
    left_root,
    right_root,
    owner_plan,
    new_left,
    new_right,
    dir_out,
    plan,
    tab_v,
    tab,
    own,
    sib,
    rs_send,
    rs_recv,
    total,
    roots,
    olds,
    send_a,
    recv_a,
    swap_b,
    send_b,
    recv_b,
    Lp,
    Rs,
    Gb,
    Rb,
    g_s,
    right_sum,
    T_s,
    D_s,
    swap_r,
    send_r,
    recv_r,
    swap_l,
    send_l,
    recv_l0,
    recv_l1,
    send_dr,
    recv_dr,
    send_dl,
    recv_dl,
    Db,
    own_sem,
    root_sem,
    old_sem,
    plan_sem,
    tab_sem,
    sib_ss,
    sib_rs,
    rs_ss,
    rs_rs,
    aa_ss,
    aa_rs,
    sw_ss,
    sw_rs,
    ex_ss,
    ex_rs,
    ag_ss,
    ag_rs,
):
    NZ, H, NF, FX, FY, STEPS = d.NZ, d.H, d.NF, d.FX, d.FY, d.STEPS
    r, f = lax.axis_index("rep"), lax.axis_index("fsdp")
    z, c = lax.div(r, 2), lax.rem(r, 2)
    y, x = lax.div(f, FX), lax.rem(f, FX)
    q = lax.rem(f, 2)
    up, down = lax.rem(z + 1, NZ) * 2 + c, lax.rem(z + NZ - 1, NZ) * 2 + c
    sibling = z * 2 + 1 - c
    partner = f + 1 - 2 * q

    around = [lax.rem(z + k, NZ) for k in range(NZ)]

    def zat(dist):
        return around[dist % NZ]

    def remote(src, dst, ss, rs, **where):
        return pltpu.make_async_remote_copy(
            src_ref=src, dst_ref=dst, send_sem=ss, recv_sem=rs, device_id=where, device_id_type=MESH
        )

    order = [H]
    for k in range(H - 1, 0, -1):
        order += [k, NZ - k]
    order += [0]

    def own_copy(k):
        return pltpu.make_async_copy(grad.at[:, c, zat(k)], own.at[k], own_sem.at[k])

    def root_copy(m):
        return pltpu.make_async_copy((left_root, right_root)[m], roots.at[m], root_sem.at[m])

    def old_copy(m, s):
        return pltpu.make_async_copy((old_left, old_right)[m].at[s], olds.at[m, s], old_sem.at[m, s])

    plan_copy = pltpu.make_async_copy(owner_plan, plan, plan_sem)
    tab_copy = pltpu.make_async_copy(tab_v, tab, tab_sem)

    barrier = pltpu.get_barrier_semaphore()

    ys = [lax.rem(y + k, FY) * FX for k in range(FY)]
    xs = [lax.rem(x + k, FX) for k in range(FX)]
    peers = [ys[i // FX] + xs[i % FX] for i in range(1, NF)]
    for where in ({"rep": sibling}, {"rep": up}, {"rep": down}, {"rep": sibling, "fsdp": partner}):
        pl.semaphore_signal(barrier, inc=1, device_id=where, device_id_type=MESH)
    for peer in peers:
        pl.semaphore_signal(barrier, inc=1, device_id={"fsdp": peer}, device_id_type=MESH)
    for k in order:
        own_copy(k).start()
    for m in range(2):
        root_copy(m).start()
    plan_copy.start()
    pl.semaphore_wait(barrier, NF - 1 + 4)

    def cut(value, piece):
        rg, cg = piece // d.CG, piece % d.CG
        return value[rg * d.PR : (rg + 1) * d.PR, cg * d.PC : (cg + 1) * d.PC]

    def cast_root(m):
        root_copy(m).wait()

        def go(s, carry):
            value = roots[m, s].astype(BF16)
            for piece in range(NF):
                send_a[piece * d.SLOTS + s, m] = cut(value, piece)
            return carry

        lax.fori_loop(0, d.SLOTS, go, 0)

    layers, columns = plan.shape
    blocks = layers * columns

    def tables():
        plan_copy.wait()
        owner = [plan[b // columns, b % columns] for b in range(blocks)]
        row = lax.broadcasted_iota(jnp.int32, (blocks, 128), 0)
        lane = lax.broadcasted_iota(jnp.int32, (blocks, 128), 1)
        owners = jnp.zeros((blocks, 128), jnp.int32)
        for b in range(blocks):
            owners = jnp.where(row == b, owner[b], owners)
        index = owners * d.SLOTS
        for b in range(blocks - 1):
            index = index + jnp.where((row > b) & (owners == owner[b]), 1, 0)
        places = jnp.zeros((blocks, 128), jnp.int32)
        for b in range(blocks):
            l, j = b // columns, b % columns
            places = jnp.where(row == b, (2 * j + l // 2) * 2 + l % 2, places)
        held = jnp.max(jnp.where(index == lane, places, -1), axis=0, keepdims=True)
        tab_v[0:blocks] = index
        tab_v[blocks : blocks + 8] = jnp.broadcast_to(held, (8, 128))
        tab_copy.start()

    def sib_copy(i, k):
        return remote(
            grad.at[:, 1 - c, zat(k), :, pl.ds(i * d.CH, d.CH)],
            sib.at[i, k],
            sib_ss.at[i],
            sib_rs.at[i, k],
            rep=sibling,
        )

    def rs_items(stream):
        items = [(H, stream)]
        for k in range(H - 1, 0, -1):
            items += [(k, 1 - stream), (k, stream)]
        return items

    def rs_slot(stream, dist, half):
        items = rs_items(stream)
        return items.index((dist, half)) if (dist, half) in items else None

    def rs_copy(i, stream, k):
        return remote(
            rs_send.at[i, stream, k],
            rs_recv.at[i, stream, k],
            rs_ss.at[i, stream],
            rs_rs.at[i, stream, k],
            rep=(up, down)[stream],
        )

    ready = set()

    def base(i, k, half):
        if k not in ready:
            own_copy(k).wait()
            ready.add(k)
        if (i, k) not in ready:
            sib_copy(i, k).wait_recv()
            ready.add((i, k))
        mine = own[k, half, :, i * d.CH : (i + 1) * d.CH]
        return mine.astype(F32) + sib[i, k, half].astype(F32)

    def rs_step(i, *steps):
        for k in steps:
            if k >= STEPS:
                continue
            for stream in range(2):
                dist, half = rs_items(stream)[k]
                value = base(i, dist if stream == 0 else NZ - dist, half)
                before = rs_slot(stream, dist + 1, half)
                if before is not None:
                    rs_copy(i, stream, before).wait_recv()
                    value = value + rs_recv[i, stream, before].astype(F32)
                rs_send[i, stream, k] = value.astype(BF16)
                rs_copy(i, stream, k).start()

    def ex_g(i):
        return remote(total.at[i, 1 - q], Gb.at[i, z, q], ex_ss.at[i], ex_rs.at[i], fsdp=partner)

    def rs_last(i):
        for half in range(2):
            value = base(i, 0, half)
            for stream in range(2):
                k = rs_slot(stream, 1, half)
                rs_copy(i, stream, k).wait_recv()
                value = value + rs_recv[i, stream, k].astype(F32)
            total[i, half] = (value / d.NR).astype(BF16)
        ex_g(i).start()
        Gb[i, z, q] = total[i, q]

    def aa_start(phase, send, recv):
        size = recv.shape[0] // NF
        part = recv.at[pl.ds(f * size, size)]
        sems = aa_ss.at[phase], aa_rs.at[phase]
        for to in peers:
            remote(send.at[pl.ds(to * size, size)], part, *sems, fsdp=to).start()
        recv[pl.ds(f * size, size)] = send[pl.ds(f * size, size)]

    def aa_all(phase, send, recv):
        most = pl.ds(0, recv.shape[0] // NF * (NF - 1))
        return remote(send.at[most], recv.at[most], aa_ss.at[phase], aa_rs.at[phase], fsdp=partner)

    def aa_wait(phase, send, recv):
        aa_all(phase, send, recv).wait_recv()

    def aa_done(phase, send, recv):
        aa_all(phase, send, recv).wait_send()

    def ag_items(stream):
        items = []
        for k in range(H - 1):
            items += [(k, stream), (k, 1 - stream)]
        return items + [(H - 1, stream)]

    bufs = (Gb.at[0], Gb.at[1], Rb)

    def ag_copy(a, stream, k, ahead):
        dist, half = ag_items(stream)[k]
        part = bufs[a].at[zat(-dist - ahead if stream == 0 else dist + ahead), half]
        return remote(part, part, ag_ss.at[a], ag_rs.at[a, stream, k], rep=(up, down)[stream])

    def ag_own(a):
        for k in range(2):
            for stream in range(2):
                ag_copy(a, stream, k, 0).start()

    def ag_step(a, *steps):
        for k in steps:
            if k >= STEPS:
                continue
            for stream in range(2):
                ag_copy(a, stream, k, 1).wait_recv()
                if k + 2 < STEPS:
                    ag_copy(a, stream, k + 2, 0).start()

    def ag_done(a):
        part = bufs[a].at[pl.ds(0, STEPS)]
        remote(part, part, ag_ss.at[a], ag_rs.at[a, 0, 0], rep=up).wait_send()

    wide = 2 * d.SR

    swap_roots = remote(swap_b, send_b.at[:, c], sw_ss.at[0], sw_rs.at[0], rep=sibling)

    def pick_roots():
        def go(p, carry):
            for core, to in ((1 - c, 0), (c, 1)):
                where = tab[(lax.rem(p, 2) * 2 + core) * columns + lax.div(p, 2), 0]
                for m in range(2):
                    value = recv_a[where, m]
                    if to == 0:
                        swap_b[p, m] = value
                    else:
                        send_b[p, c, m] = value
            return carry

        lax.fori_loop(0, NF, go, 0)
        swap_roots.start()

    def join_roots():
        for piece in range(NF):
            rg, cg = piece // d.CG, piece % d.CG
            cols = pl.ds(cg * d.PC, d.PC)
            for core in range(2):
                Lp[pl.ds(core * d.SR + rg * d.PR, d.PR), cols] = recv_b[piece, core, 0]
                Rs[pl.ds(core * d.SR + rg * d.PR, d.PR), cols] = recv_b[piece, core, 1]
        for dist in range(H + 1):
            at = pl.multiple_of(zat(dist) * wide, wide)
            for core in range(2):
                Rb[z, core, :, dist * wide : (dist + 1) * wide] = Rs[
                    core * d.SR : (core + 1) * d.SR, pl.ds(at, wide)
                ]

    def block(i, half):
        return Gb[i, :, half].reshape(d.BLK, d.CH)

    near_first = [0]
    for k in range(1, H):
        near_first += [k, -k]
    near_first += [H]
    groups = near_first[: NZ // 2], near_first[NZ // 2 :]
    swaps, sends, takes = (
        (swap_l.at[0], swap_l.at[1], swap_r),
        (send_l.at[0], send_l.at[1], send_r),
        (recv_l0, recv_l1, recv_r),
    )
    backs = (
        (send_dl.at[0], recv_dl.at[0]),
        (send_dl.at[1], recv_dl.at[1]),
        (send_dr, recv_dr),
    )
    span = d.BLK // 2

    def swap_gram(m):
        return remote(swaps[m], sends[m].at[:, c], sw_ss.at[1 + m], sw_rs.at[1 + m], rep=sibling)

    def put_gram(m):
        width = d.PC if m == 2 else wide
        for core, mine in ((1 - c, False), (c, True)):
            value = g_s[1, core] if m == 2 else g_s[0, core, :, m * span : (m + 1) * span]
            for piece in range(NF):
                rg, cg = piece // d.CG, piece % d.CG
                part = value[rg * d.PR : (rg + 1) * d.PR, cg * width : (cg + 1) * width]
                if mine:
                    sends[m][piece, c] = part
                else:
                    swaps[m][piece] = part
            if not mine:
                swap_gram(m).start()

    def near(group, i, half, *cols):
        return jnp.concatenate([Gb[i, zat(k), half, :, *cols] for k in groups[group]], axis=0)

    def gram_left(group):
        value = 0.0
        for i in range(2):
            for h in range(2):
                value = value + lax.dot_general(
                    Gb[i, z, h],
                    near(group, i, h),
                    (((1,), (1,)), ((), ())),
                    preferred_element_type=F32,
                )
        value = ((1.0 - gram_decay) * value).astype(BF16)
        g_s[0, :, :, group * span : (group + 1) * span] = value.reshape(2, d.SR, span)
        put_gram(group)

    def gram_right(group):
        at = z * wide
        half, rest = lax.div(at, d.HC), lax.rem(at, d.HC)
        chain, off = lax.div(rest, d.CH), lax.rem(rest, d.CH)
        cols = near(group, chain, half, pl.ds(pl.multiple_of(off, wide), wide))
        for i in range(2):
            for h in range(2):
                both = lax.dot_general(
                    cols, near(group, i, h), (((0,), (0,)), ((), ())), preferred_element_type=F32
                )
                first = h * d.HC + i * d.CH
                if group == 0:
                    right_sum[:, first : first + d.CH] = both
                else:
                    both = both + right_sum[:, first : first + d.CH]
                    both = ((1.0 - gram_decay) * both).astype(BF16)
                    g_s[1, :, :, first : first + d.CH] = both.reshape(2, d.SR, d.CH)
        if group == 1:
            put_gram(2)

    def left_times(i):
        for h in range(2):
            first = h * d.HC + i * d.CH
            value = jnp.dot(Lp[...], block(i, h), preferred_element_type=F32).astype(BF16)
            for t in range(d.CH // wide):
                T_s[first // wide + t] = value[:, t * wide : (t + 1) * wide]

    def spread(m):
        swap_gram(m).wait_recv()
        aa_start(2 + m, sends[m], takes[m])

    def give_back(m):
        aa_wait(2 + m, sends[m], takes[m])
        send, recv = backs[m]

        def go(o, carry):
            for s in range(d.SLOTS):
                where = jnp.maximum(tab[blocks, o * d.SLOTS + s], 0)
                send[o * d.SLOTS + s] = takes[m][lax.div(where, 2), lax.rem(where, 2)]
            return carry

        lax.fori_loop(0, NF, go, 0)
        aa_start(5 + m, send, recv)

    def add_grams(m):
        send, recv = backs[m]
        aa_wait(5 + m, send, recv)
        side = m // 2
        if m != 1:
            for s in range(d.SLOTS):
                old_copy(side, s).wait()

        def go(s, carry):
            live = tab[blocks, f * d.SLOTS + s] >= 0
            for piece in range(NF):
                rg, cg = piece // d.CG, piece % d.CG
                rows = pl.ds(rg * d.PR, d.PR)
                if m == 2:
                    cols = pl.ds(cg * d.PC, d.PC)
                else:
                    cols = pl.ds(pl.multiple_of(zat(groups[m][cg]) * wide, wide), wide)
                added = jnp.where(live, recv[piece * d.SLOTS + s].astype(F32), 0.0)
                (new_left, new_right)[side][s, rows, cols] = (
                    gram_decay * olds[side, s, rows, cols] + added
                )
            return carry

        lax.fori_loop(0, d.SLOTS, go, 0)

    homes = (
        remote(Db.at[c, 1 - q], dir_out.at[q, c], ex_ss.at[2], ex_rs.at[2], fsdp=partner),
        remote(Db.at[1 - c, q], dir_out.at[q, c], ex_ss.at[3], ex_rs.at[3], rep=sibling),
        remote(
            Db.at[1 - c, 1 - q], dir_out.at[q, c], ex_ss.at[4], ex_rs.at[4], rep=sibling, fsdp=partner
        ),
    )

    def add_slab(dist):
        k = zat(dist)
        root = Rb[k].reshape(wide, (H + 1) * wide)
        direct = jnp.dot(T_s[k], root, preferred_element_type=F32)
        for t in range(H + 1):
            D_s[zat(dist + t)] += direct[:, t * wide : (t + 1) * wide]
        turned = jnp.concatenate([T_s[zat(dist + t)] for t in range(1, H)], axis=1)
        D_s[k] += lax.dot_general(
            turned, root[:, wide : H * wide], (((1,), (1,)), ((), ())), preferred_element_type=F32
        )

    def directions():
        for k in range(NZ):
            value = D_s[k].astype(BF16).reshape(2, d.SR, wide)
            half, at = divmod(k * wide, d.HC)
            Db[:, half, :, at : at + wide] = value
        for copy in homes:
            copy.start()
        dir_out[q, c] = Db[c, q]

    def fetch_old(s):
        for m in range(2):
            old_copy(m, s).start()

    for k in order[:3]:
        sib_copy(0, k).start()
    rs_step(0, 0)
    for k in order[3:]:
        sib_copy(0, k).start()
    rs_step(0, 1)
    for k in order:
        sib_copy(1, k).start()
    rs_step(1, 0)
    cast_root(0)
    rs_step(0, 2)
    rs_step(1, 1)
    cast_root(1)
    aa_start(0, send_a, recv_a)
    rs_step(0, 3)
    rs_step(1, 2)
    tables()
    rs_step(0, 4)
    rs_step(1, 3)
    rs_step(0, 5)
    rs_step(1, 4)
    rs_step(0, 6)
    rs_step(1, 5)
    rs_last(0)
    rs_step(1, 6)
    ex_g(0).wait_recv()
    ag_own(0)
    rs_last(1)
    ag_step(0, 0)
    ex_g(1).wait_recv()
    ag_own(1)
    ag_step(0, 1)
    aa_wait(0, send_a, recv_a)
    tab_copy.wait()
    pick_roots()
    ag_step(0, 2)
    ag_step(1, 0)
    swap_roots.wait_recv()
    aa_start(1, send_b, recv_b)
    ag_step(0, 3)
    ag_step(1, 1)
    fetch_old(0)
    ag_step(0, 4)
    ag_step(1, 2)
    fetch_old(1)
    ag_step(0, 5)
    ag_step(1, 3)
    fetch_old(2)
    gram_left(0)
    ag_step(0, 6)
    ag_step(1, 4)
    fetch_old(3)
    spread(0)
    gram_right(0)
    aa_wait(1, send_b, recv_b)
    join_roots()
    ag_own(2)
    give_back(0)
    ag_step(1, 5, 6)
    gram_right(1)
    gram_left(1)
    ag_step(2, 0)
    spread(2)
    spread(1)
    ag_step(2, 1)
    left_times(0)
    give_back(2)
    ag_step(2, 2)
    give_back(1)
    ag_step(2, 3)
    left_times(1)
    D_s[...] = jnp.zeros_like(D_s)
    add_slab(0)
    ag_step(2, 4)
    for dist in range(1, min(3, H)):
        add_slab(-dist)
        add_slab(dist)

    for i in range(2):
        remote(sib.at[i], sib.at[i], sib_ss.at[i], sib_rs.at[i, 0], rep=sibling).wait_send()
        for stream in range(2):
            sent = rs_send.at[i, stream]
            remote(sent, sent, rs_ss.at[i, stream], rs_rs.at[i, stream, 0], rep=up).wait_send()
        ex_g(i).wait_send()
        ag_done(i)
    aa_done(0, send_a, recv_a)
    aa_done(1, send_b, recv_b)
    swap_roots.wait_send()
    for m in range(3):
        swap_gram(m).wait_send()
        aa_done(2 + m, sends[m], takes[m])
    aa_done(5, *backs[0])
    add_grams(0)

    ag_step(2, 5)
    for dist in range(3, H):
        add_slab(-dist)
        add_slab(dist)
    ag_step(2, 6)
    add_slab(H)
    directions()
    add_grams(2)
    add_grams(1)
    ag_done(2)
    for m in range(1, 3):
        aa_done(5 + m, *backs[m])
    for copy in homes:
        copy.wait()


def local(gradients, old_left, old_right, left_root, right_root, owner_plan):
    rep, fsdp = lax.axis_size("rep"), lax.axis_size("fsdp")
    _, layers, rows, home = gradients.shape
    slots = old_left.shape[0]
    d = Dims(rep, fsdp, layers, rows, home, slots)

    S, NZ, NF = d.STEPS, d.NZ, d.NF
    CR = 2 * d.SR
    piece = (d.PR, d.PC)
    vmem = lambda *shape: pltpu.VMEM(shape, BF16)
    wide = lambda *shape: pltpu.VMEM(shape, F32)
    dma = lambda *shape: pltpu.SemaphoreType.DMA(shape)
    whole = pl.BlockSpec(memory_space=pltpu.VMEM)
    away = pl.BlockSpec(memory_space=pl.ANY)
    new_left, new_right, direction = pl.pallas_call(
        functools.partial(kernel, d),
        out_shape=(
            jax.ShapeDtypeStruct(old_left.shape, F32),
            jax.ShapeDtypeStruct(old_right.shape, F32),
            jax.ShapeDtypeStruct((2, 2, d.SR, d.HC), BF16),
        ),
        in_specs=[away] * 6,
        out_specs=(whole,) * 3,
        scratch_shapes=[
            pltpu.SMEM(owner_plan.shape, jnp.int32),
            pltpu.VMEM((owner_plan.size + 8, 128), jnp.int32),
            pltpu.SMEM((owner_plan.size + 8, 128), jnp.int32),
            vmem(NZ, 2, CR, d.HC),
            vmem(2, NZ, 2, CR, d.CH),
            vmem(2, 2, S, CR, d.CH),
            vmem(2, 2, S, CR, d.CH),
            vmem(2, 2, CR, d.CH),
            wide(2, slots, d.SR, d.BLK),
            wide(2, slots, d.SR, d.BLK),
            vmem(NF * slots, 2, *piece),
            vmem(NF * slots, 2, *piece),
            vmem(NF, 2, *piece),
            vmem(NF, 2, 2, *piece),
            vmem(NF, 2, 2, *piece),
            vmem(CR, d.BLK),
            vmem(CR, d.BLK),
            vmem(2, NZ, 2, CR, d.CH),
            vmem(NZ, 2, d.SR, (d.H + 1) * CR),
            vmem(2, 2, d.SR, d.BLK),
            wide(CR, d.BLK),
            vmem(NZ, CR, CR),
            wide(NZ, CR, CR),
            vmem(NF, *piece),
            vmem(NF, 2, *piece),
            vmem(NF, 2, *piece),
            vmem(2, NF, d.PR, CR),
            vmem(2, NF, 2, d.PR, CR),
            vmem(NF, 2, d.PR, CR),
            vmem(NF, 2, d.PR, CR),
            vmem(NF * slots, *piece),
            vmem(NF * slots, *piece),
            vmem(2, NF * slots, d.PR, CR),
            vmem(2, NF * slots, d.PR, CR),
            vmem(2, 2, d.SR, d.HC),
            dma(NZ),
            dma(2),
            dma(2, slots),
            pltpu.SemaphoreType.DMA,
            pltpu.SemaphoreType.DMA,
            dma(2),
            dma(2, NZ),
            dma(2, 2),
            dma(2, 2, S),
            dma(8),
            dma(8),
            dma(4),
            dma(4),
            dma(5),
            dma(5),
            dma(3),
            dma(3, 2, S),
        ],
        compiler_params=pltpu.CompilerParams(
            collective_id=0, has_side_effects=True, vmem_limit_bytes=51 * 1024 * 1024
        ),
        cost_estimate=pl.CostEstimate(
            flops=2 * 5 * 2 * d.SR * d.BLK * d.BLK,
            bytes_accessed=2 * gradients.size + 24 * left_root.size,
            transcendentals=0,
        ),
    )(
        gradients.reshape(2, 2, NZ, CR, home),
        old_left,
        old_right,
        left_root,
        right_root,
        owner_plan,
    )
    return new_left, new_right, direction.reshape(layers, d.SR, home)


def solution(mesh):
    return jax.shard_map(
        local,
        mesh=mesh,
        in_specs=(
            P("rep", None, None, "fsdp"),
            P("fsdp", "rep", None),
            P("fsdp", "rep", None),
            P("fsdp", "rep", None),
            P("fsdp", "rep", None),
            P(),
        ),
        out_specs=(P("fsdp", "rep", None), P("fsdp", "rep", None), P(None, "rep", "fsdp")),
        check_vma=False,
    )
```

```python
import functools

import jax
import jax.numpy as jnp
from jax import lax
from jax.experimental import pallas as pl
from jax.experimental.pallas import tpu as pltpu
from jax.sharding import PartitionSpec as P

gram_decay = 0.95
MESH = pl.DeviceIdType.MESH
F32 = jnp.float32
BF16 = jnp.bfloat16


class Dims:
    def __init__(self, rep, fsdp, layers, rows, home, slots):
        self.NR, self.NF, self.NZ = rep, fsdp, rep // 2
        self.FX = 4 if fsdp == 16 else 2
        self.FY = fsdp // self.FX
        self.H = self.NZ // 2
        self.STEPS = 2 * self.H - 1
        self.BLK = rows
        self.SR = rows // rep
        self.HC = home
        self.CH = home // 2
        self.SLOTS = slots
        self.CG = 4 if fsdp == 16 else 2
        self.RG = fsdp // self.CG
        self.PR, self.PC = self.SR // self.RG, rows // self.CG


def kernel(
    d,
    grad,
    old_left,
    old_right,
    left_root,
    right_root,
    owner_plan,
    new_left,
    new_right,
    dir_out,
    plan,
    tab_v,
    tab,
    own,
    sib,
    rs_send,
    rs_recv,
    total,
    roots,
    olds,
    send_a,
    recv_a0,
    recv_a1,
    swap_b,
    send_b,
    recv_b,
    Lp,
    Rs,
    Gb,
    Rb,
    g_s,
    right_sum,
    T_s,
    D_s,
    swap_r,
    send_r,
    recv_r,
    swap_l,
    send_l,
    recv_l0,
    recv_l1,
    send_dr,
    recv_dr,
    send_dl,
    recv_dl,
    Db,
    own_sem,
    root_sem,
    old_sem,
    plan_sem,
    tab_sem,
    sib_ss,
    sib_rs,
    rs_ss,
    rs_rs,
    aa_ss,
    aa_rs,
    sw_ss,
    sw_rs,
    ex_ss,
    ex_rs,
    ag_ss,
    ag_rs,
):
    NZ, H, NF, FX, FY, STEPS = d.NZ, d.H, d.NF, d.FX, d.FY, d.STEPS
    r, f = lax.axis_index("rep"), lax.axis_index("fsdp")
    z, c = lax.div(r, 2), lax.rem(r, 2)
    y, x = lax.div(f, FX), lax.rem(f, FX)
    q = lax.rem(f, 2)
    up, down = lax.rem(z + 1, NZ) * 2 + c, lax.rem(z + NZ - 1, NZ) * 2 + c
    sibling = z * 2 + 1 - c
    partner = f + 1 - 2 * q

    around = [lax.rem(z + k, NZ) for k in range(NZ)]

    def zat(dist):
        return around[dist % NZ]

    def remote(src, dst, ss, rs, **where):
        return pltpu.make_async_remote_copy(
            src_ref=src, dst_ref=dst, send_sem=ss, recv_sem=rs, device_id=where, device_id_type=MESH
        )

    order = [H]
    for k in range(H - 1, 0, -1):
        order += [k, NZ - k]
    order += [0]

    def own_copy(k):
        return pltpu.make_async_copy(grad.at[:, c, zat(k)], own.at[k], own_sem.at[k])

    def root_copy(m):
        return pltpu.make_async_copy((left_root, right_root)[m], roots.at[m], root_sem.at[m])

    def old_copy(m, s):
        return pltpu.make_async_copy((old_left, old_right)[m].at[s], olds.at[m, s], old_sem.at[m, s])

    plan_copy = pltpu.make_async_copy(owner_plan, plan, plan_sem)
    tab_copy = pltpu.make_async_copy(tab_v, tab, tab_sem)

    barrier = pltpu.get_barrier_semaphore()

    ys = [lax.rem(y + k, FY) * FX for k in range(FY)]
    xs = [lax.rem(x + k, FX) for k in range(FX)]
    peers = [ys[i // FX] + xs[i % FX] for i in range(1, NF)]
    for where in ({"rep": sibling}, {"rep": up}, {"rep": down}, {"rep": sibling, "fsdp": partner}):
        pl.semaphore_signal(barrier, inc=1, device_id=where, device_id_type=MESH)
    for peer in peers:
        pl.semaphore_signal(barrier, inc=1, device_id={"fsdp": peer}, device_id_type=MESH)
    for k in order[:3]:
        own_copy(k).start()
    root_copy(1).start()
    root_copy(0).start()
    plan_copy.start()
    for k in order[3:]:
        own_copy(k).start()
    pl.semaphore_wait(barrier, NF - 1 + 4)

    def cut(value, piece):
        rg, cg = piece // d.CG, piece % d.CG
        return value[rg * d.PR : (rg + 1) * d.PR, cg * d.PC : (cg + 1) * d.PC]

    def cast_root(m):
        root_copy(m).wait()

        def go(s, carry):
            value = roots[m, s].astype(BF16)
            for piece in range(NF):
                send_a[m, piece * d.SLOTS + s] = cut(value, piece)
            return carry

        lax.fori_loop(0, d.SLOTS, go, 0)

    layers, columns = plan.shape
    blocks = layers * columns

    def tables():
        plan_copy.wait()
        owner = [plan[b // columns, b % columns] for b in range(blocks)]
        row = lax.broadcasted_iota(jnp.int32, (blocks, 128), 0)
        lane = lax.broadcasted_iota(jnp.int32, (blocks, 128), 1)
        owners = jnp.zeros((blocks, 128), jnp.int32)
        for b in range(blocks):
            owners = jnp.where(row == b, owner[b], owners)
        index = owners * d.SLOTS
        for b in range(blocks - 1):
            index = index + jnp.where((row > b) & (owners == owner[b]), 1, 0)
        places = jnp.zeros((blocks, 128), jnp.int32)
        for b in range(blocks):
            l, j = b // columns, b % columns
            places = jnp.where(row == b, (2 * j + l // 2) * 2 + l % 2, places)
        held = jnp.max(jnp.where(index == lane, places, -1), axis=0, keepdims=True)
        tab_v[0:blocks] = index
        tab_v[blocks : blocks + 8] = jnp.broadcast_to(held, (8, 128))
        tab_copy.start()

    def sib_copy(i, k):
        return remote(
            grad.at[:, 1 - c, zat(k), :, pl.ds(i * d.CH, d.CH)],
            sib.at[i, k],
            sib_ss.at[i],
            sib_rs.at[i, k],
            rep=sibling,
        )

    def rs_items(stream):
        items = [(H, stream)]
        for k in range(H - 1, 0, -1):
            items += [(k, 1 - stream), (k, stream)]
        return items

    def rs_slot(stream, dist, half):
        items = rs_items(stream)
        return items.index((dist, half)) if (dist, half) in items else None

    def rs_copy(i, stream, k):
        return remote(
            rs_send.at[i, stream, k],
            rs_recv.at[i, stream, k],
            rs_ss.at[i, stream],
            rs_rs.at[i, stream, k],
            rep=(up, down)[stream],
        )

    ready = set()

    def base(i, k, half):
        if k not in ready:
            own_copy(k).wait()
            ready.add(k)
        if (i, k) not in ready:
            sib_copy(i, k).wait_recv()
            ready.add((i, k))
        mine = own[k, half, :, i * d.CH : (i + 1) * d.CH]
        return mine.astype(F32) + sib[i, k, half].astype(F32)

    def rs_step(i, *steps):
        for k in steps:
            if k >= STEPS:
                continue
            for stream in range(2):
                dist, half = rs_items(stream)[k]
                value = base(i, dist if stream == 0 else NZ - dist, half)
                before = rs_slot(stream, dist + 1, half)
                if before is not None:
                    rs_copy(i, stream, before).wait_recv()
                    value = value + rs_recv[i, stream, before].astype(F32)
                rs_send[i, stream, k] = value.astype(BF16)
                rs_copy(i, stream, k).start()

    def ex_g(i):
        return remote(total.at[i, 1 - q], Gb.at[i, z, q], ex_ss.at[i], ex_rs.at[i], fsdp=partner)

    def rs_last(i):
        for half in range(2):
            value = base(i, 0, half)
            for stream in range(2):
                k = rs_slot(stream, 1, half)
                rs_copy(i, stream, k).wait_recv()
                value = value + rs_recv[i, stream, k].astype(F32)
            total[i, half] = (value / d.NR).astype(BF16)
        ex_g(i).start()
        Gb[i, z, q] = total[i, q]

    def aa_start(phase, send, recv):
        size = recv.shape[0] // NF
        part = recv.at[pl.ds(f * size, size)]
        sems = aa_ss.at[phase], aa_rs.at[phase]
        for to in peers:
            remote(send.at[pl.ds(to * size, size)], part, *sems, fsdp=to).start()
        recv[pl.ds(f * size, size)] = send[pl.ds(f * size, size)]

    def aa_all(phase, send, recv):
        most = pl.ds(0, recv.shape[0] // NF * (NF - 1))
        return remote(send.at[most], recv.at[most], aa_ss.at[phase], aa_rs.at[phase], fsdp=partner)

    def aa_wait(phase, send, recv):
        aa_all(phase, send, recv).wait_recv()

    def aa_done(phase, send, recv):
        aa_all(phase, send, recv).wait_send()

    def ag_items(stream):
        items = []
        for k in range(H - 1):
            items += [(k, stream), (k, 1 - stream)]
        return items + [(H - 1, stream)]

    bufs = (Gb.at[0], Gb.at[1], Rb)

    def ag_copy(a, stream, k, ahead):
        dist, half = ag_items(stream)[k]
        part = bufs[a].at[zat(-dist - ahead if stream == 0 else dist + ahead), half]
        return remote(part, part, ag_ss.at[a], ag_rs.at[a, stream, k], rep=(up, down)[stream])

    def ag_own(a):
        for k in range(2):
            for stream in range(2):
                ag_copy(a, stream, k, 0).start()

    def ag_step(a, *steps):
        for k in steps:
            if k >= STEPS:
                continue
            for stream in range(2):
                ag_copy(a, stream, k, 1).wait_recv()
                if k + 2 < STEPS:
                    ag_copy(a, stream, k + 2, 0).start()

    def ag_done(a):
        part = bufs[a].at[pl.ds(0, STEPS)]
        remote(part, part, ag_ss.at[a], ag_rs.at[a, 0, 0], rep=up).wait_send()

    wide = 2 * d.SR

    recv_a = (recv_a0, recv_a1)

    def swap_root(m):
        return remote(swap_b.at[m], send_b.at[m, :, c], sw_ss.at[4 + m], sw_rs.at[4 + m], rep=sibling)

    def pick_root(m):
        aa_wait(m, send_a.at[m], recv_a[m])

        def go(p, carry):
            for core, mine in ((1 - c, False), (c, True)):
                where = tab[(lax.rem(p, 2) * 2 + core) * columns + lax.div(p, 2), 0]
                value = recv_a[m][where]
                if mine:
                    send_b[m, p, c] = value
                else:
                    swap_b[m, p] = value
            return carry

        lax.fori_loop(0, NF, go, 0)
        swap_root(m).start()

    def pass_root(m):
        swap_root(m).wait_recv()
        aa_start(8 + m, send_b.at[m], recv_b.at[m])

    def join_root(m):
        aa_wait(8 + m, send_b.at[m], recv_b.at[m])
        for piece in range(NF):
            rg, cg = piece // d.CG, piece % d.CG
            cols = pl.ds(cg * d.PC, d.PC)
            for core in range(2):
                at = core * d.SR + rg * d.PR
                (Lp, Rs)[m][pl.ds(at, d.PR), cols] = recv_b[m, piece, core]
        if m == 0:
            return
        for dist in range(H + 1):
            at = pl.multiple_of(zat(dist) * wide, wide)
            for core in range(2):
                Rb[z, core, :, dist * wide : (dist + 1) * wide] = Rs[
                    core * d.SR : (core + 1) * d.SR, pl.ds(at, wide)
                ]

    def block(i, half):
        return Gb[i, :, half].reshape(d.BLK, d.CH)

    near_first = [0]
    for k in range(1, H):
        near_first += [k, -k]
    near_first += [H]
    groups = near_first[: NZ // 2], near_first[NZ // 2 :]
    swaps, sends, takes = (
        (swap_l.at[0], swap_l.at[1], swap_r),
        (send_l.at[0], send_l.at[1], send_r),
        (recv_l0, recv_l1, recv_r),
    )
    backs = (
        (send_dl.at[0], recv_dl.at[0]),
        (send_dl.at[1], recv_dl.at[1]),
        (send_dr, recv_dr),
    )
    span = d.BLK // 2

    def swap_gram(m):
        return remote(swaps[m], sends[m].at[:, c], sw_ss.at[1 + m], sw_rs.at[1 + m], rep=sibling)

    def put_gram(m):
        width = d.PC if m == 2 else wide
        for core, mine in ((1 - c, False), (c, True)):
            value = g_s[1, core] if m == 2 else g_s[0, core, :, m * span : (m + 1) * span]
            for piece in range(NF):
                rg, cg = piece // d.CG, piece % d.CG
                part = value[rg * d.PR : (rg + 1) * d.PR, cg * width : (cg + 1) * width]
                if mine:
                    sends[m][piece, c] = part
                else:
                    swaps[m][piece] = part
            if not mine:
                swap_gram(m).start()

    def near(group, i, half, *cols):
        return jnp.concatenate([Gb[i, zat(k), half, :, *cols] for k in groups[group]], axis=0)

    def gram_left(group):
        value = 0.0
        for i in range(2):
            for h in range(2):
                value = value + lax.dot_general(
                    Gb[i, z, h],
                    near(group, i, h),
                    (((1,), (1,)), ((), ())),
                    preferred_element_type=F32,
                )
        value = ((1.0 - gram_decay) * value).astype(BF16)
        g_s[0, :, :, group * span : (group + 1) * span] = value.reshape(2, d.SR, span)
        put_gram(group)

    def gram_right(group):
        at = z * wide
        half, rest = lax.div(at, d.HC), lax.rem(at, d.HC)
        chain, off = lax.div(rest, d.CH), lax.rem(rest, d.CH)
        cols = near(group, chain, half, pl.ds(pl.multiple_of(off, wide), wide))
        for i in range(2):
            for h in range(2):
                both = lax.dot_general(
                    cols, near(group, i, h), (((0,), (0,)), ((), ())), preferred_element_type=F32
                )
                first = h * d.HC + i * d.CH
                if group == 0:
                    right_sum[:, first : first + d.CH] = both
                else:
                    both = both + right_sum[:, first : first + d.CH]
                    both = ((1.0 - gram_decay) * both).astype(BF16)
                    g_s[1, :, :, first : first + d.CH] = both.reshape(2, d.SR, d.CH)
        if group == 1:
            put_gram(2)

    def left_times(i):
        for h in range(2):
            first = h * d.HC + i * d.CH
            value = jnp.dot(Lp[...], block(i, h), preferred_element_type=F32).astype(BF16)
            for t in range(d.CH // wide):
                T_s[first // wide + t] = value[:, t * wide : (t + 1) * wide]

    def spread(m):
        swap_gram(m).wait_recv()
        aa_start(2 + m, sends[m], takes[m])

    def give_back(m):
        aa_wait(2 + m, sends[m], takes[m])
        send, recv = backs[m]

        def go(o, carry):
            for s in range(d.SLOTS):
                where = jnp.maximum(tab[blocks, o * d.SLOTS + s], 0)
                send[o * d.SLOTS + s] = takes[m][lax.div(where, 2), lax.rem(where, 2)]
            return carry

        lax.fori_loop(0, NF, go, 0)
        aa_start(5 + m, send, recv)

    def add_grams(m):
        send, recv = backs[m]
        aa_wait(5 + m, send, recv)
        side = m // 2
        if m != 1:
            for s in range(d.SLOTS):
                old_copy(side, s).wait()

        def go(s, carry):
            live = tab[blocks, f * d.SLOTS + s] >= 0
            for piece in range(NF):
                rg, cg = piece // d.CG, piece % d.CG
                rows = pl.ds(rg * d.PR, d.PR)
                if m == 2:
                    cols = pl.ds(cg * d.PC, d.PC)
                else:
                    cols = pl.ds(pl.multiple_of(zat(groups[m][cg]) * wide, wide), wide)
                added = jnp.where(live, recv[piece * d.SLOTS + s].astype(F32), 0.0)
                (new_left, new_right)[side][s, rows, cols] = (
                    gram_decay * olds[side, s, rows, cols] + added
                )
            return carry

        lax.fori_loop(0, d.SLOTS, go, 0)

    homes = (
        remote(Db.at[c, 1 - q], dir_out.at[q, c], ex_ss.at[2], ex_rs.at[2], fsdp=partner),
        remote(Db.at[1 - c, q], dir_out.at[q, c], ex_ss.at[3], ex_rs.at[3], rep=sibling),
        remote(
            Db.at[1 - c, 1 - q], dir_out.at[q, c], ex_ss.at[4], ex_rs.at[4], rep=sibling, fsdp=partner
        ),
    )

    def add_slab(dist):
        k = zat(dist)
        root = Rb[k].reshape(wide, (H + 1) * wide)
        direct = jnp.dot(T_s[k], root, preferred_element_type=F32)
        for t in range(H + 1):
            D_s[zat(dist + t)] += direct[:, t * wide : (t + 1) * wide]
        turned = jnp.concatenate([T_s[zat(dist + t)] for t in range(1, H)], axis=1)
        D_s[k] += lax.dot_general(
            turned, root[:, wide : H * wide], (((1,), (1,)), ((), ())), preferred_element_type=F32
        )

    def directions():
        for k in range(NZ):
            value = D_s[k].astype(BF16).reshape(2, d.SR, wide)
            half, at = divmod(k * wide, d.HC)
            Db[:, half, :, at : at + wide] = value
        for copy in homes:
            copy.start()
        dir_out[q, c] = Db[c, q]

    def fetch_old(s):
        for m in range(2):
            old_copy(m, s).start()

    for k in order[:3]:
        sib_copy(0, k).start()
    rs_step(0, 0)
    for k in order[3:]:
        sib_copy(0, k).start()
    rs_step(0, 1)
    for k in order:
        sib_copy(1, k).start()
    rs_step(1, 0)
    cast_root(1)
    aa_start(1, send_a.at[1], recv_a1)
    rs_step(0, 2)
    rs_step(1, 1)
    cast_root(0)
    aa_start(0, send_a.at[0], recv_a0)
    rs_step(0, 3)
    rs_step(1, 2)
    tables()
    rs_step(0, 4)
    rs_step(1, 3)
    rs_step(0, 5)
    rs_step(1, 4)
    tab_copy.wait()
    pick_root(1)
    rs_step(0, 6)
    rs_step(1, 5)
    pass_root(1)
    rs_last(0)
    rs_step(1, 6)
    ex_g(0).wait_recv()
    ag_own(0)
    rs_last(1)
    ag_step(0, 0)
    ex_g(1).wait_recv()
    ag_own(1)
    ag_step(0, 1)
    ag_step(0, 2)
    ag_step(1, 0)
    pick_root(0)
    ag_step(0, 3)
    ag_step(1, 1)
    fetch_old(0)
    pass_root(0)
    ag_step(0, 4)
    ag_step(1, 2)
    fetch_old(1)
    ag_step(0, 5)
    ag_step(1, 3)
    fetch_old(2)
    gram_left(0)
    ag_step(0, 6)
    ag_step(1, 4)
    fetch_old(3)
    spread(0)
    gram_right(0)
    join_root(1)
    ag_own(2)
    give_back(0)
    ag_step(1, 5, 6)
    gram_right(1)
    gram_left(1)
    ag_step(2, 0)
    spread(2)
    spread(1)
    ag_step(2, 1)
    join_root(0)
    left_times(0)
    give_back(2)
    ag_step(2, 2)
    give_back(1)
    ag_step(2, 3)
    left_times(1)
    D_s[...] = jnp.zeros_like(D_s)
    add_slab(0)
    ag_step(2, 4)
    for dist in range(1, min(3, H)):
        add_slab(-dist)
        add_slab(dist)

    for i in range(2):
        remote(sib.at[i], sib.at[i], sib_ss.at[i], sib_rs.at[i, 0], rep=sibling).wait_send()
        for stream in range(2):
            sent = rs_send.at[i, stream]
            remote(sent, sent, rs_ss.at[i, stream], rs_rs.at[i, stream, 0], rep=up).wait_send()
        ex_g(i).wait_send()
        ag_done(i)
    for m in range(2):
        aa_done(m, send_a.at[m], recv_a[m])
        aa_done(8 + m, send_b.at[m], recv_b.at[m])
        swap_root(m).wait_send()
    for m in range(3):
        swap_gram(m).wait_send()
        aa_done(2 + m, sends[m], takes[m])
    aa_done(5, *backs[0])
    add_grams(0)

    ag_step(2, 5)
    for dist in range(3, H):
        add_slab(-dist)
        add_slab(dist)
    ag_step(2, 6)
    add_slab(H)
    directions()
    add_grams(2)
    add_grams(1)
    ag_done(2)
    for m in range(1, 3):
        aa_done(5 + m, *backs[m])
    for copy in homes:
        copy.wait()


def local(gradients, old_left, old_right, left_root, right_root, owner_plan):
    rep, fsdp = lax.axis_size("rep"), lax.axis_size("fsdp")
    _, layers, rows, home = gradients.shape
    slots = old_left.shape[0]
    d = Dims(rep, fsdp, layers, rows, home, slots)

    S, NZ, NF = d.STEPS, d.NZ, d.NF
    CR = 2 * d.SR
    piece = (d.PR, d.PC)
    vmem = lambda *shape: pltpu.VMEM(shape, BF16)
    wide = lambda *shape: pltpu.VMEM(shape, F32)
    dma = lambda *shape: pltpu.SemaphoreType.DMA(shape)
    whole = pl.BlockSpec(memory_space=pltpu.VMEM)
    away = pl.BlockSpec(memory_space=pl.ANY)
    new_left, new_right, direction = pl.pallas_call(
        functools.partial(kernel, d),
        out_shape=(
            jax.ShapeDtypeStruct(old_left.shape, F32),
            jax.ShapeDtypeStruct(old_right.shape, F32),
            jax.ShapeDtypeStruct((2, 2, d.SR, d.HC), BF16),
        ),
        in_specs=[away] * 6,
        out_specs=(whole,) * 3,
        scratch_shapes=[
            pltpu.SMEM(owner_plan.shape, jnp.int32),
            pltpu.VMEM((owner_plan.size + 8, 128), jnp.int32),
            pltpu.SMEM((owner_plan.size + 8, 128), jnp.int32),
            vmem(NZ, 2, CR, d.HC),
            vmem(2, NZ, 2, CR, d.CH),
            vmem(2, 2, S, CR, d.CH),
            vmem(2, 2, S, CR, d.CH),
            vmem(2, 2, CR, d.CH),
            wide(2, slots, d.SR, d.BLK),
            wide(2, slots, d.SR, d.BLK),
            vmem(2, NF * slots, *piece),
            vmem(NF * slots, *piece),
            vmem(NF * slots, *piece),
            vmem(2, NF, *piece),
            vmem(2, NF, 2, *piece),
            vmem(2, NF, 2, *piece),
            vmem(CR, d.BLK),
            vmem(CR, d.BLK),
            vmem(2, NZ, 2, CR, d.CH),
            vmem(NZ, 2, d.SR, (d.H + 1) * CR),
            vmem(2, 2, d.SR, d.BLK),
            wide(CR, d.BLK),
            vmem(NZ, CR, CR),
            wide(NZ, CR, CR),
            vmem(NF, *piece),
            vmem(NF, 2, *piece),
            vmem(NF, 2, *piece),
            vmem(2, NF, d.PR, CR),
            vmem(2, NF, 2, d.PR, CR),
            vmem(NF, 2, d.PR, CR),
            vmem(NF, 2, d.PR, CR),
            vmem(NF * slots, *piece),
            vmem(NF * slots, *piece),
            vmem(2, NF * slots, d.PR, CR),
            vmem(2, NF * slots, d.PR, CR),
            vmem(2, 2, d.SR, d.HC),
            dma(NZ),
            dma(2),
            dma(2, slots),
            pltpu.SemaphoreType.DMA,
            pltpu.SemaphoreType.DMA,
            dma(2),
            dma(2, NZ),
            dma(2, 2),
            dma(2, 2, S),
            dma(10),
            dma(10),
            dma(6),
            dma(6),
            dma(5),
            dma(5),
            dma(3),
            dma(3, 2, S),
        ],
        compiler_params=pltpu.CompilerParams(
            collective_id=0, has_side_effects=True, vmem_limit_bytes=51 * 1024 * 1024
        ),
        cost_estimate=pl.CostEstimate(
            flops=2 * 5 * 2 * d.SR * d.BLK * d.BLK,
            bytes_accessed=2 * gradients.size + 24 * left_root.size,
            transcendentals=0,
        ),
    )(
        gradients.reshape(2, 2, NZ, CR, home),
        old_left,
        old_right,
        left_root,
        right_root,
        owner_plan,
    )
    return new_left, new_right, direction.reshape(layers, d.SR, home)


def solution(mesh):
    return jax.shard_map(
        local,
        mesh=mesh,
        in_specs=(
            P("rep", None, None, "fsdp"),
            P("fsdp", "rep", None),
            P("fsdp", "rep", None),
            P("fsdp", "rep", None),
            P("fsdp", "rep", None),
            P(),
        ),
        out_specs=(P("fsdp", "rep", None), P("fsdp", "rep", None), P(None, "rep", "fsdp")),
        check_vma=False,
    )
```

```python
import functools

import jax
import jax.numpy as jnp
from jax import lax
from jax.experimental import pallas as pl
from jax.experimental.pallas import tpu as pltpu
from jax.sharding import PartitionSpec as P

gram_decay = 0.95
MESH = pl.DeviceIdType.MESH
F32 = jnp.float32
BF16 = jnp.bfloat16


class Dims:
    def __init__(self, rep, fsdp, layers, rows, home, slots):
        self.NR, self.NF, self.NZ = rep, fsdp, rep // 2
        self.FX = 4 if fsdp == 16 else 2
        self.FY = fsdp // self.FX
        self.H = self.NZ // 2
        self.STEPS = 2 * self.H - 1
        self.BLK = rows
        self.SR = rows // rep
        self.HC = home
        self.CH = home // 2
        self.SLOTS = slots
        self.CG = 4 if fsdp == 16 else 2
        self.RG = fsdp // self.CG
        self.PR, self.PC = self.SR // self.RG, rows // self.CG


def kernel(
    d,
    grad,
    old_left,
    old_right,
    left_root,
    right_root,
    owner_plan,
    new_left,
    new_right,
    dir_out,
    plan,
    tab_v,
    tab,
    own,
    sib,
    rs_send,
    rs_recv,
    total,
    roots,
    olds,
    send_a,
    recv_a0,
    recv_a1,
    swap_b,
    send_b,
    recv_b,
    Lp,
    Rs,
    Gb,
    Rb,
    g_s,
    right_sum,
    T_s,
    D_s,
    swap_r,
    send_r,
    recv_r,
    swap_l,
    send_l,
    recv_l0,
    recv_l1,
    send_dr,
    recv_dr,
    send_dl,
    recv_dl,
    Db,
    own_sem,
    root_sem,
    old_sem,
    plan_sem,
    tab_sem,
    sib_ss,
    sib_rs,
    rs_ss,
    rs_rs,
    aa_ss,
    aa_rs,
    sw_ss,
    sw_rs,
    ex_ss,
    ex_rs,
    ag_ss,
    ag_rs,
):
    NZ, H, NF, FX, FY, STEPS = d.NZ, d.H, d.NF, d.FX, d.FY, d.STEPS
    r, f = lax.axis_index("rep"), lax.axis_index("fsdp")
    z, c = lax.div(r, 2), lax.rem(r, 2)
    y, x = lax.div(f, FX), lax.rem(f, FX)
    q = lax.rem(f, 2)
    up, down = lax.rem(z + 1, NZ) * 2 + c, lax.rem(z + NZ - 1, NZ) * 2 + c
    sibling = z * 2 + 1 - c
    partner = f + 1 - 2 * q

    around = [lax.rem(z + k, NZ) for k in range(NZ)]

    def zat(dist):
        return around[dist % NZ]

    def remote(src, dst, ss, rs, **where):
        return pltpu.make_async_remote_copy(
            src_ref=src, dst_ref=dst, send_sem=ss, recv_sem=rs, device_id=where, device_id_type=MESH
        )

    order = [H]
    for k in range(H - 1, 0, -1):
        order += [k, NZ - k]
    order += [0]

    def own_copy(k):
        return pltpu.make_async_copy(grad.at[:, c, zat(k)], own.at[k], own_sem.at[k])

    def root_copy(m):
        return pltpu.make_async_copy((left_root, right_root)[m], roots.at[m], root_sem.at[m])

    def old_copy(m, s):
        return pltpu.make_async_copy((old_left, old_right)[m].at[s], olds.at[m, s], old_sem.at[m, s])

    plan_copy = pltpu.make_async_copy(owner_plan, plan, plan_sem)
    tab_copy = pltpu.make_async_copy(tab_v, tab, tab_sem)

    barrier = pltpu.get_barrier_semaphore()

    ys = [lax.rem(y + k, FY) * FX for k in range(FY)]
    xs = [lax.rem(x + k, FX) for k in range(FX)]
    peers = [ys[i // FX] + xs[i % FX] for i in range(1, NF)]
    for where in ({"rep": sibling}, {"rep": up}, {"rep": down}, {"rep": sibling, "fsdp": partner}):
        pl.semaphore_signal(barrier, inc=1, device_id=where, device_id_type=MESH)
    for peer in peers:
        pl.semaphore_signal(barrier, inc=1, device_id={"fsdp": peer}, device_id_type=MESH)
    for k in order[:3]:
        own_copy(k).start()
    root_copy(1).start()
    root_copy(0).start()
    plan_copy.start()
    for k in order[3:]:
        own_copy(k).start()
    pl.semaphore_wait(barrier, NF - 1 + 4)

    def cut(value, piece):
        rg, cg = piece // d.CG, piece % d.CG
        return value[rg * d.PR : (rg + 1) * d.PR, cg * d.PC : (cg + 1) * d.PC]

    def cast_root(m):
        root_copy(m).wait()

        def go(s, carry):
            value = roots[m, s].astype(BF16)
            for piece in range(NF):
                send_a[m, piece * d.SLOTS + s] = cut(value, piece)
            return carry

        lax.fori_loop(0, d.SLOTS, go, 0)

    layers, columns = plan.shape
    blocks = layers * columns

    def tables():
        plan_copy.wait()
        owner = [plan[b // columns, b % columns] for b in range(blocks)]
        row = lax.broadcasted_iota(jnp.int32, (blocks, 128), 0)
        lane = lax.broadcasted_iota(jnp.int32, (blocks, 128), 1)
        owners = jnp.zeros((blocks, 128), jnp.int32)
        for b in range(blocks):
            owners = jnp.where(row == b, owner[b], owners)
        index = owners * d.SLOTS
        for b in range(blocks - 1):
            index = index + jnp.where((row > b) & (owners == owner[b]), 1, 0)
        places = jnp.zeros((blocks, 128), jnp.int32)
        for b in range(blocks):
            l, j = b // columns, b % columns
            places = jnp.where(row == b, (2 * j + l // 2) * 2 + l % 2, places)
        held = jnp.max(jnp.where(index == lane, places, -1), axis=0, keepdims=True)
        tab_v[0:blocks] = index
        tab_v[blocks : blocks + 8] = jnp.broadcast_to(held, (8, 128))
        tab_copy.start()

    def sib_copy(i, k):
        return remote(
            grad.at[:, 1 - c, zat(k), :, pl.ds(i * d.CH, d.CH)],
            sib.at[i, k],
            sib_ss.at[i],
            sib_rs.at[i, k],
            rep=sibling,
        )

    def rs_items(stream):
        items = [(H, stream)]
        for k in range(H - 1, 0, -1):
            items += [(k, 1 - stream), (k, stream)]
        return items

    def rs_slot(stream, dist, half):
        items = rs_items(stream)
        return items.index((dist, half)) if (dist, half) in items else None

    def rs_copy(i, stream, k):
        return remote(
            rs_send.at[i, stream, k],
            rs_recv.at[i, stream, k],
            rs_ss.at[i, stream],
            rs_rs.at[i, stream, k],
            rep=(up, down)[stream],
        )

    ready = set()

    def base(i, k, half):
        if k not in ready:
            own_copy(k).wait()
            ready.add(k)
        if (i, k) not in ready:
            sib_copy(i, k).wait_recv()
            ready.add((i, k))
        mine = own[k, half, :, i * d.CH : (i + 1) * d.CH]
        return mine.astype(F32) + sib[i, k, half].astype(F32)

    def rs_step(i, *steps):
        for k in steps:
            if k >= STEPS:
                continue
            for stream in range(2):
                dist, half = rs_items(stream)[k]
                value = base(i, dist if stream == 0 else NZ - dist, half)
                before = rs_slot(stream, dist + 1, half)
                if before is not None:
                    rs_copy(i, stream, before).wait_recv()
                    value = value + rs_recv[i, stream, before].astype(F32)
                rs_send[i, stream, k] = value.astype(BF16)
                rs_copy(i, stream, k).start()

    def ex_g(i):
        return remote(total.at[i, 1 - q], Gb.at[i, z, q], ex_ss.at[i], ex_rs.at[i], fsdp=partner)

    def rs_last(i):
        for half in range(2):
            value = base(i, 0, half)
            for stream in range(2):
                k = rs_slot(stream, 1, half)
                rs_copy(i, stream, k).wait_recv()
                value = value + rs_recv[i, stream, k].astype(F32)
            total[i, half] = (value / d.NR).astype(BF16)
        ex_g(i).start()
        Gb[i, z, q] = total[i, q]

    def aa_start(phase, send, recv):
        size = recv.shape[0] // NF
        part = recv.at[pl.ds(f * size, size)]
        sems = aa_ss.at[phase], aa_rs.at[phase]
        for to in peers:
            remote(send.at[pl.ds(to * size, size)], part, *sems, fsdp=to).start()
        recv[pl.ds(f * size, size)] = send[pl.ds(f * size, size)]

    def aa_all(phase, send, recv):
        most = pl.ds(0, recv.shape[0] // NF * (NF - 1))
        return remote(send.at[most], recv.at[most], aa_ss.at[phase], aa_rs.at[phase], fsdp=partner)

    def aa_wait(phase, send, recv):
        aa_all(phase, send, recv).wait_recv()

    def aa_done(phase, send, recv):
        aa_all(phase, send, recv).wait_send()

    def ag_items(stream):
        items = []
        for k in range(H - 1):
            items += [(k, stream), (k, 1 - stream)]
        return items + [(H - 1, stream)]

    bufs = (Gb.at[0], Gb.at[1], Rb)

    def ag_copy(a, stream, k, ahead):
        dist, half = ag_items(stream)[k]
        part = bufs[a].at[zat(-dist - ahead if stream == 0 else dist + ahead), half]
        return remote(part, part, ag_ss.at[a], ag_rs.at[a, stream, k], rep=(up, down)[stream])

    def ag_own(a):
        for k in range(2):
            for stream in range(2):
                ag_copy(a, stream, k, 0).start()

    def ag_step(a, *steps):
        for k in steps:
            if k >= STEPS:
                continue
            for stream in range(2):
                ag_copy(a, stream, k, 1).wait_recv()
                if k + 2 < STEPS:
                    ag_copy(a, stream, k + 2, 0).start()

    def ag_done(a):
        part = bufs[a].at[pl.ds(0, STEPS)]
        remote(part, part, ag_ss.at[a], ag_rs.at[a, 0, 0], rep=up).wait_send()

    wide = 2 * d.SR

    recv_a = (recv_a0, recv_a1)

    def swap_root(m):
        return remote(swap_b.at[m], send_b.at[m, :, c], sw_ss.at[4 + m], sw_rs.at[4 + m], rep=sibling)

    def pick_root(m):
        aa_wait(m, send_a.at[m], recv_a[m])

        def go(p, carry):
            for core, mine in ((1 - c, False), (c, True)):
                where = tab[(lax.rem(p, 2) * 2 + core) * columns + lax.div(p, 2), 0]
                value = recv_a[m][where]
                if mine:
                    send_b[m, p, c] = value
                else:
                    swap_b[m, p] = value
            return carry

        lax.fori_loop(0, NF, go, 0)
        swap_root(m).start()

    def pass_root(m):
        swap_root(m).wait_recv()
        aa_start(8 + m, send_b.at[m], recv_b.at[m])

    def join_root(m):
        aa_wait(8 + m, send_b.at[m], recv_b.at[m])
        for piece in range(NF):
            rg, cg = piece // d.CG, piece % d.CG
            cols = pl.ds(cg * d.PC, d.PC)
            for core in range(2):
                at = core * d.SR + rg * d.PR
                (Lp, Rs)[m][pl.ds(at, d.PR), cols] = recv_b[m, piece, core]
        if m == 0:
            return
        for dist in range(H + 1):
            at = pl.multiple_of(zat(dist) * wide, wide)
            for core in range(2):
                Rb[z, core, :, dist * wide : (dist + 1) * wide] = Rs[
                    core * d.SR : (core + 1) * d.SR, pl.ds(at, wide)
                ]

    def block(i, half):
        return Gb[i, :, half].reshape(d.BLK, d.CH)

    near_first = [0]
    for k in range(1, H):
        near_first += [k, -k]
    near_first += [H]
    groups = near_first[: NZ // 2], near_first[NZ // 2 :]
    swaps, sends, takes = (
        (swap_l.at[0], swap_l.at[1], swap_r),
        (send_l.at[0], send_l.at[1], send_r),
        (recv_l0, recv_l1, recv_r),
    )
    backs = (
        (send_dl.at[0], recv_dl.at[0]),
        (send_dl.at[1], recv_dl.at[1]),
        (send_dr, recv_dr),
    )
    span = d.BLK // 2

    def swap_gram(m):
        return remote(swaps[m], sends[m].at[:, c], sw_ss.at[1 + m], sw_rs.at[1 + m], rep=sibling)

    def put_gram(m):
        width = d.PC if m == 2 else wide
        for core, mine in ((1 - c, False), (c, True)):
            value = g_s[1, core] if m == 2 else g_s[0, core, :, m * span : (m + 1) * span]
            for piece in range(NF):
                rg, cg = piece // d.CG, piece % d.CG
                part = value[rg * d.PR : (rg + 1) * d.PR, cg * width : (cg + 1) * width]
                if mine:
                    sends[m][piece, c] = part
                else:
                    swaps[m][piece] = part
            if not mine:
                swap_gram(m).start()

    def near(group, i, half, *cols):
        return jnp.concatenate([Gb[i, zat(k), half, :, *cols] for k in groups[group]], axis=0)

    def gram_left(group):
        value = 0.0
        for i in range(2):
            for h in range(2):
                value = value + lax.dot_general(
                    Gb[i, z, h],
                    near(group, i, h),
                    (((1,), (1,)), ((), ())),
                    preferred_element_type=F32,
                )
        value = ((1.0 - gram_decay) * value).astype(BF16)
        g_s[0, :, :, group * span : (group + 1) * span] = value.reshape(2, d.SR, span)
        put_gram(group)

    def gram_right(group):
        at = z * wide
        half, rest = lax.div(at, d.HC), lax.rem(at, d.HC)
        chain, off = lax.div(rest, d.CH), lax.rem(rest, d.CH)
        cols = near(group, chain, half, pl.ds(pl.multiple_of(off, wide), wide))
        for i in range(2):
            for h in range(2):
                both = lax.dot_general(
                    cols, near(group, i, h), (((0,), (0,)), ((), ())), preferred_element_type=F32
                )
                first = h * d.HC + i * d.CH
                if group == 0:
                    right_sum[:, first : first + d.CH] = both
                else:
                    both = both + right_sum[:, first : first + d.CH]
                    both = ((1.0 - gram_decay) * both).astype(BF16)
                    g_s[1, :, :, first : first + d.CH] = both.reshape(2, d.SR, d.CH)
        if group == 1:
            put_gram(2)

    def left_times(i):
        for h in range(2):
            first = h * d.HC + i * d.CH
            value = jnp.dot(Lp[...], block(i, h), preferred_element_type=F32).astype(BF16)
            for t in range(d.CH // wide):
                T_s[first // wide + t] = value[:, t * wide : (t + 1) * wide]

    def spread(m):
        swap_gram(m).wait_recv()
        aa_start(2 + m, sends[m], takes[m])

    def give_back(m):
        aa_wait(2 + m, sends[m], takes[m])
        send, recv = backs[m]

        def go(o, carry):
            for s in range(d.SLOTS):
                where = jnp.maximum(tab[blocks, o * d.SLOTS + s], 0)
                send[o * d.SLOTS + s] = takes[m][lax.div(where, 2), lax.rem(where, 2)]
            return carry

        lax.fori_loop(0, NF, go, 0)
        aa_start(5 + m, send, recv)

    def add_grams(m):
        send, recv = backs[m]
        aa_wait(5 + m, send, recv)
        side = m // 2
        if m != 1:
            for s in range(d.SLOTS):
                old_copy(side, s).wait()

        def go(s, carry):
            live = tab[blocks, f * d.SLOTS + s] >= 0
            for piece in range(NF):
                rg, cg = piece // d.CG, piece % d.CG
                rows = pl.ds(rg * d.PR, d.PR)
                if m == 2:
                    cols = pl.ds(cg * d.PC, d.PC)
                else:
                    cols = pl.ds(pl.multiple_of(zat(groups[m][cg]) * wide, wide), wide)
                added = jnp.where(live, recv[piece * d.SLOTS + s].astype(F32), 0.0)
                (new_left, new_right)[side][s, rows, cols] = (
                    gram_decay * olds[side, s, rows, cols] + added
                )
            return carry

        lax.fori_loop(0, d.SLOTS, go, 0)

    homes = (
        remote(Db.at[c, 1 - q], dir_out.at[q, c], ex_ss.at[2], ex_rs.at[2], fsdp=partner),
        remote(Db.at[1 - c, q], dir_out.at[q, c], ex_ss.at[3], ex_rs.at[3], rep=sibling),
        remote(
            Db.at[1 - c, 1 - q], dir_out.at[q, c], ex_ss.at[4], ex_rs.at[4], rep=sibling, fsdp=partner
        ),
    )

    def add_slab(dist):
        k = zat(dist)
        root = Rb[k].reshape(wide, (H + 1) * wide)
        direct = jnp.dot(T_s[k], root, preferred_element_type=F32)
        for t in range(H + 1):
            D_s[zat(dist + t)] += direct[:, t * wide : (t + 1) * wide]
        turned = jnp.concatenate([T_s[zat(dist + t)] for t in range(1, H)], axis=1)
        D_s[k] += lax.dot_general(
            turned, root[:, wide : H * wide], (((1,), (1,)), ((), ())), preferred_element_type=F32
        )

    def directions():
        for k in range(NZ):
            value = D_s[k].astype(BF16).reshape(2, d.SR, wide)
            half, at = divmod(k * wide, d.HC)
            Db[:, half, :, at : at + wide] = value
        for copy in homes:
            copy.start()
        dir_out[q, c] = Db[c, q]

    def fetch_old(s):
        for m in range(2):
            old_copy(m, s).start()

    for k in order[:3]:
        sib_copy(0, k).start()
    rs_step(0, 0)
    for k in order[3:]:
        sib_copy(0, k).start()
    rs_step(0, 1)
    for k in order:
        sib_copy(1, k).start()
    rs_step(1, 0)
    cast_root(1)
    aa_start(1, send_a.at[1], recv_a1)
    rs_step(0, 2, 3)
    cast_root(0)
    aa_start(0, send_a.at[0], recv_a0)
    rs_step(1, 1)
    tables()
    rs_step(0, 4, 5)
    rs_step(1, 2)
    rs_step(0, 6)
    rs_step(1, 3)
    tab_copy.wait()
    pick_root(1)
    rs_step(1, 4)
    rs_last(0)
    rs_step(1, 5)
    pass_root(1)
    rs_step(1, 6)
    ex_g(0).wait_recv()
    ag_own(0)
    rs_last(1)
    ag_step(0, 0)
    ex_g(1).wait_recv()
    ag_own(1)
    ag_step(0, 1)
    ag_step(0, 2)
    ag_step(1, 0)
    pick_root(0)
    ag_step(0, 3)
    ag_step(1, 1)
    fetch_old(0)
    pass_root(0)
    ag_step(0, 4)
    ag_step(1, 2)
    fetch_old(1)
    ag_step(0, 5)
    ag_step(1, 3)
    fetch_old(2)
    gram_left(0)
    ag_step(0, 6)
    ag_step(1, 4)
    fetch_old(3)
    spread(0)
    gram_right(0)
    join_root(1)
    ag_own(2)
    give_back(0)
    ag_step(1, 5, 6)
    gram_right(1)
    gram_left(1)
    ag_step(2, 0)
    spread(2)
    spread(1)
    ag_step(2, 1)
    join_root(0)
    left_times(0)
    give_back(2)
    ag_step(2, 2)
    give_back(1)
    ag_step(2, 3)
    left_times(1)
    D_s[...] = jnp.zeros_like(D_s)
    add_slab(0)
    ag_step(2, 4)
    for dist in range(1, min(3, H)):
        add_slab(-dist)
        add_slab(dist)

    for i in range(2):
        remote(sib.at[i], sib.at[i], sib_ss.at[i], sib_rs.at[i, 0], rep=sibling).wait_send()
        for stream in range(2):
            sent = rs_send.at[i, stream]
            remote(sent, sent, rs_ss.at[i, stream], rs_rs.at[i, stream, 0], rep=up).wait_send()
        ex_g(i).wait_send()
        ag_done(i)
    for m in range(2):
        aa_done(m, send_a.at[m], recv_a[m])
        aa_done(8 + m, send_b.at[m], recv_b.at[m])
        swap_root(m).wait_send()
    for m in range(3):
        swap_gram(m).wait_send()
        aa_done(2 + m, sends[m], takes[m])
    aa_done(5, *backs[0])
    add_grams(0)

    ag_step(2, 5)
    for dist in range(3, H):
        add_slab(-dist)
        add_slab(dist)
    ag_step(2, 6)
    add_slab(H)
    directions()
    add_grams(2)
    add_grams(1)
    ag_done(2)
    for m in range(1, 3):
        aa_done(5 + m, *backs[m])
    for copy in homes:
        copy.wait()


def local(gradients, old_left, old_right, left_root, right_root, owner_plan):
    rep, fsdp = lax.axis_size("rep"), lax.axis_size("fsdp")
    _, layers, rows, home = gradients.shape
    slots = old_left.shape[0]
    d = Dims(rep, fsdp, layers, rows, home, slots)

    S, NZ, NF = d.STEPS, d.NZ, d.NF
    CR = 2 * d.SR
    piece = (d.PR, d.PC)
    vmem = lambda *shape: pltpu.VMEM(shape, BF16)
    wide = lambda *shape: pltpu.VMEM(shape, F32)
    dma = lambda *shape: pltpu.SemaphoreType.DMA(shape)
    whole = pl.BlockSpec(memory_space=pltpu.VMEM)
    away = pl.BlockSpec(memory_space=pl.ANY)
    new_left, new_right, direction = pl.pallas_call(
        functools.partial(kernel, d),
        out_shape=(
            jax.ShapeDtypeStruct(old_left.shape, F32),
            jax.ShapeDtypeStruct(old_right.shape, F32),
            jax.ShapeDtypeStruct((2, 2, d.SR, d.HC), BF16),
        ),
        in_specs=[away] * 6,
        out_specs=(whole,) * 3,
        scratch_shapes=[
            pltpu.SMEM(owner_plan.shape, jnp.int32),
            pltpu.VMEM((owner_plan.size + 8, 128), jnp.int32),
            pltpu.SMEM((owner_plan.size + 8, 128), jnp.int32),
            vmem(NZ, 2, CR, d.HC),
            vmem(2, NZ, 2, CR, d.CH),
            vmem(2, 2, S, CR, d.CH),
            vmem(2, 2, S, CR, d.CH),
            vmem(2, 2, CR, d.CH),
            wide(2, slots, d.SR, d.BLK),
            wide(2, slots, d.SR, d.BLK),
            vmem(2, NF * slots, *piece),
            vmem(NF * slots, *piece),
            vmem(NF * slots, *piece),
            vmem(2, NF, *piece),
            vmem(2, NF, 2, *piece),
            vmem(2, NF, 2, *piece),
            vmem(CR, d.BLK),
            vmem(CR, d.BLK),
            vmem(2, NZ, 2, CR, d.CH),
            vmem(NZ, 2, d.SR, (d.H + 1) * CR),
            vmem(2, 2, d.SR, d.BLK),
            wide(CR, d.BLK),
            vmem(NZ, CR, CR),
            wide(NZ, CR, CR),
            vmem(NF, *piece),
            vmem(NF, 2, *piece),
            vmem(NF, 2, *piece),
            vmem(2, NF, d.PR, CR),
            vmem(2, NF, 2, d.PR, CR),
            vmem(NF, 2, d.PR, CR),
            vmem(NF, 2, d.PR, CR),
            vmem(NF * slots, *piece),
            vmem(NF * slots, *piece),
            vmem(2, NF * slots, d.PR, CR),
            vmem(2, NF * slots, d.PR, CR),
            vmem(2, 2, d.SR, d.HC),
            dma(NZ),
            dma(2),
            dma(2, slots),
            pltpu.SemaphoreType.DMA,
            pltpu.SemaphoreType.DMA,
            dma(2),
            dma(2, NZ),
            dma(2, 2),
            dma(2, 2, S),
            dma(10),
            dma(10),
            dma(6),
            dma(6),
            dma(5),
            dma(5),
            dma(3),
            dma(3, 2, S),
        ],
        compiler_params=pltpu.CompilerParams(
            collective_id=0, has_side_effects=True, vmem_limit_bytes=51 * 1024 * 1024
        ),
        cost_estimate=pl.CostEstimate(
            flops=2 * 5 * 2 * d.SR * d.BLK * d.BLK,
            bytes_accessed=2 * gradients.size + 24 * left_root.size,
            transcendentals=0,
        ),
    )(
        gradients.reshape(2, 2, NZ, CR, home),
        old_left,
        old_right,
        left_root,
        right_root,
        owner_plan,
    )
    return new_left, new_right, direction.reshape(layers, d.SR, home)


def solution(mesh):
    return jax.shard_map(
        local,
        mesh=mesh,
        in_specs=(
            P("rep", None, None, "fsdp"),
            P("fsdp", "rep", None),
            P("fsdp", "rep", None),
            P("fsdp", "rep", None),
            P("fsdp", "rep", None),
            P(),
        ),
        out_specs=(P("fsdp", "rep", None), P("fsdp", "rep", None), P(None, "rep", "fsdp")),
        check_vma=False,
    )
```

```python
import functools

import jax
import jax.numpy as jnp
from jax import lax
from jax.experimental import pallas as pl
from jax.experimental.pallas import tpu as pltpu
from jax.sharding import PartitionSpec as P

gram_decay = 0.95
MESH = pl.DeviceIdType.MESH
F32 = jnp.float32
BF16 = jnp.bfloat16


class Dims:
    def __init__(self, rep, fsdp, layers, rows, home, slots):
        self.NR, self.NF, self.NZ = rep, fsdp, rep // 2
        self.FX = 4 if fsdp == 16 else 2
        self.FY = fsdp // self.FX
        self.H = self.NZ // 2
        self.STEPS = 2 * self.H - 1
        self.BLK = rows
        self.SR = rows // rep
        self.HC = home
        self.CH = home // 2
        self.SLOTS = slots
        self.CG = 4 if fsdp == 16 else 2
        self.RG = fsdp // self.CG
        self.PR, self.PC = self.SR // self.RG, rows // self.CG


def kernel(
    d,
    grad,
    old_left,
    old_right,
    left_root,
    right_root,
    owner_plan,
    new_left,
    new_right,
    dir_out,
    plan,
    tab_v,
    tab,
    own,
    sib,
    rs_send,
    rs_recv,
    total,
    roots,
    olds,
    send_a,
    recv_a0,
    recv_a1,
    swap_b,
    send_b,
    recv_b,
    Lp,
    Rs,
    Gb,
    Rb,
    g_s,
    right_sum,
    T_s,
    D_s,
    swap_r,
    send_r,
    recv_r,
    swap_l,
    send_l,
    recv_l0,
    recv_l1,
    send_dr,
    recv_dr,
    send_dl,
    recv_dl,
    Db,
    own_sem,
    root_sem,
    old_sem,
    plan_sem,
    tab_sem,
    sib_ss,
    sib_rs,
    rs_ss,
    rs_rs,
    aa_ss,
    aa_rs,
    sw_ss,
    sw_rs,
    ex_ss,
    ex_rs,
    ag_ss,
    ag_rs,
):
    NZ, H, NF, FX, FY, STEPS = d.NZ, d.H, d.NF, d.FX, d.FY, d.STEPS
    r, f = lax.axis_index("rep"), lax.axis_index("fsdp")
    z, c = lax.div(r, 2), lax.rem(r, 2)
    y, x = lax.div(f, FX), lax.rem(f, FX)
    q = lax.rem(f, 2)
    up, down = lax.rem(z + 1, NZ) * 2 + c, lax.rem(z + NZ - 1, NZ) * 2 + c
    sibling = z * 2 + 1 - c
    partner = f + 1 - 2 * q

    around = [lax.rem(z + k, NZ) for k in range(NZ)]

    def zat(dist):
        return around[dist % NZ]

    def remote(src, dst, ss, rs, **where):
        return pltpu.make_async_remote_copy(
            src_ref=src, dst_ref=dst, send_sem=ss, recv_sem=rs, device_id=where, device_id_type=MESH
        )

    order = [H]
    for k in range(H - 1, 0, -1):
        order += [k, NZ - k]
    order += [0]

    def own_copy(k):
        return pltpu.make_async_copy(grad.at[:, c, zat(k)], own.at[k], own_sem.at[k])

    def root_copy(m):
        return pltpu.make_async_copy((left_root, right_root)[m], roots.at[m], root_sem.at[m])

    def old_copy(m, s):
        return pltpu.make_async_copy((old_left, old_right)[m].at[s], olds.at[m, s], old_sem.at[m, s])

    plan_copy = pltpu.make_async_copy(owner_plan, plan, plan_sem)
    tab_copy = pltpu.make_async_copy(tab_v, tab, tab_sem)

    barrier = pltpu.get_barrier_semaphore()

    ys = [lax.rem(y + k, FY) * FX for k in range(FY)]
    xs = [lax.rem(x + k, FX) for k in range(FX)]
    peers = [ys[i // FX] + xs[i % FX] for i in range(1, NF)]
    for where in ({"rep": sibling}, {"rep": up}, {"rep": down}, {"rep": sibling, "fsdp": partner}):
        pl.semaphore_signal(barrier, inc=1, device_id=where, device_id_type=MESH)
    for peer in peers:
        pl.semaphore_signal(barrier, inc=1, device_id={"fsdp": peer}, device_id_type=MESH)
    for k in order[:3]:
        own_copy(k).start()
    root_copy(1).start()
    root_copy(0).start()
    plan_copy.start()
    for k in order[3:]:
        own_copy(k).start()
    pl.semaphore_wait(barrier, NF - 1 + 4)

    def cut(value, piece):
        rg, cg = piece // d.CG, piece % d.CG
        return value[rg * d.PR : (rg + 1) * d.PR, cg * d.PC : (cg + 1) * d.PC]

    def cast_root(m):
        root_copy(m).wait()

        def go(s, carry):
            value = roots[m, s].astype(BF16)
            for piece in range(NF):
                send_a[m, piece * d.SLOTS + s] = cut(value, piece)
            return carry

        lax.fori_loop(0, d.SLOTS, go, 0)

    layers, columns = plan.shape
    blocks = layers * columns

    def tables():
        plan_copy.wait()
        owner = [plan[b // columns, b % columns] for b in range(blocks)]
        row = lax.broadcasted_iota(jnp.int32, (blocks, 128), 0)
        lane = lax.broadcasted_iota(jnp.int32, (blocks, 128), 1)
        owners = jnp.zeros((blocks, 128), jnp.int32)
        for b in range(blocks):
            owners = jnp.where(row == b, owner[b], owners)
        index = owners * d.SLOTS
        for b in range(blocks - 1):
            index = index + jnp.where((row > b) & (owners == owner[b]), 1, 0)
        places = jnp.zeros((blocks, 128), jnp.int32)
        for b in range(blocks):
            l, j = b // columns, b % columns
            places = jnp.where(row == b, (2 * j + l // 2) * 2 + l % 2, places)
        held = jnp.max(jnp.where(index == lane, places, -1), axis=0, keepdims=True)
        tab_v[0:blocks] = index
        tab_v[blocks : blocks + 8] = jnp.broadcast_to(held, (8, 128))
        tab_copy.start()

    def sib_copy(i, k):
        return remote(
            grad.at[:, 1 - c, zat(k), :, pl.ds(i * d.CH, d.CH)],
            sib.at[i, k],
            sib_ss.at[i],
            sib_rs.at[i, k],
            rep=sibling,
        )

    def rs_items(stream):
        items = [(H, stream)]
        for k in range(H - 1, 0, -1):
            items += [(k, 1 - stream), (k, stream)]
        return items

    def rs_slot(stream, dist, half):
        items = rs_items(stream)
        return items.index((dist, half)) if (dist, half) in items else None

    def rs_copy(i, stream, k):
        return remote(
            rs_send.at[i, stream, k],
            rs_recv.at[i, stream, k],
            rs_ss.at[i, stream],
            rs_rs.at[i, stream, k],
            rep=(up, down)[stream],
        )

    ready = set()

    def base(i, k, half):
        if k not in ready:
            own_copy(k).wait()
            ready.add(k)
        if (i, k) not in ready:
            sib_copy(i, k).wait_recv()
            ready.add((i, k))
        mine = own[k, half, :, i * d.CH : (i + 1) * d.CH]
        return mine.astype(F32) + sib[i, k, half].astype(F32)

    def rs_step(i, *steps):
        for k in steps:
            if k >= STEPS:
                continue
            for stream in range(2):
                dist, half = rs_items(stream)[k]
                value = base(i, dist if stream == 0 else NZ - dist, half)
                before = rs_slot(stream, dist + 1, half)
                if before is not None:
                    rs_copy(i, stream, before).wait_recv()
                    value = value + rs_recv[i, stream, before].astype(F32)
                rs_send[i, stream, k] = value.astype(BF16)
                rs_copy(i, stream, k).start()

    def ex_g(i):
        return remote(total.at[i, 1 - q], Gb.at[i, z, q], ex_ss.at[i], ex_rs.at[i], fsdp=partner)

    def rs_last(i):
        for half in range(2):
            value = base(i, 0, half)
            for stream in range(2):
                k = rs_slot(stream, 1, half)
                rs_copy(i, stream, k).wait_recv()
                value = value + rs_recv[i, stream, k].astype(F32)
            total[i, half] = (value / d.NR).astype(BF16)
        ex_g(i).start()
        Gb[i, z, q] = total[i, q]

    def aa_start(phase, send, recv):
        size = recv.shape[0] // NF
        part = recv.at[pl.ds(f * size, size)]
        sems = aa_ss.at[phase], aa_rs.at[phase]
        for to in peers:
            remote(send.at[pl.ds(to * size, size)], part, *sems, fsdp=to).start()
        recv[pl.ds(f * size, size)] = send[pl.ds(f * size, size)]

    def aa_all(phase, send, recv):
        most = pl.ds(0, recv.shape[0] // NF * (NF - 1))
        return remote(send.at[most], recv.at[most], aa_ss.at[phase], aa_rs.at[phase], fsdp=partner)

    def aa_wait(phase, send, recv):
        aa_all(phase, send, recv).wait_recv()

    def aa_done(phase, send, recv):
        aa_all(phase, send, recv).wait_send()

    def ag_items(stream):
        items = []
        for k in range(H - 1):
            items += [(k, stream), (k, 1 - stream)]
        return items + [(H - 1, stream)]

    bufs = (Gb.at[0], Gb.at[1], Rb)

    def ag_copy(a, stream, k, ahead):
        dist, half = ag_items(stream)[k]
        part = bufs[a].at[zat(-dist - ahead if stream == 0 else dist + ahead), half]
        return remote(part, part, ag_ss.at[a], ag_rs.at[a, stream, k], rep=(up, down)[stream])

    def ag_own(a):
        for k in range(2):
            for stream in range(2):
                ag_copy(a, stream, k, 0).start()

    def ag_step(a, *steps):
        for k in steps:
            if k >= STEPS:
                continue
            for stream in range(2):
                ag_copy(a, stream, k, 1).wait_recv()
                if k + 2 < STEPS:
                    ag_copy(a, stream, k + 2, 0).start()

    def ag_done(a):
        part = bufs[a].at[pl.ds(0, STEPS)]
        remote(part, part, ag_ss.at[a], ag_rs.at[a, 0, 0], rep=up).wait_send()

    wide = 2 * d.SR

    recv_a = (recv_a0, recv_a1)

    def swap_root(m):
        return remote(swap_b.at[m], send_b.at[m, :, c], sw_ss.at[4 + m], sw_rs.at[4 + m], rep=sibling)

    def pick_root(m):
        aa_wait(m, send_a.at[m], recv_a[m])

        def go(p, carry):
            for core, mine in ((1 - c, False), (c, True)):
                where = tab[(lax.rem(p, 2) * 2 + core) * columns + lax.div(p, 2), 0]
                value = recv_a[m][where]
                if mine:
                    send_b[m, p, c] = value
                else:
                    swap_b[m, p] = value
            return carry

        lax.fori_loop(0, NF, go, 0)
        swap_root(m).start()

    def pass_root(m):
        swap_root(m).wait_recv()
        aa_start(8 + m, send_b.at[m], recv_b.at[m])

    def join_root(m):
        aa_wait(8 + m, send_b.at[m], recv_b.at[m])
        for piece in range(NF):
            rg, cg = piece // d.CG, piece % d.CG
            cols = pl.ds(cg * d.PC, d.PC)
            for core in range(2):
                at = core * d.SR + rg * d.PR
                (Lp, Rs)[m][pl.ds(at, d.PR), cols] = recv_b[m, piece, core]
        if m == 0:
            return
        for dist in range(H + 1):
            at = pl.multiple_of(zat(dist) * wide, wide)
            for core in range(2):
                Rb[z, core, :, dist * wide : (dist + 1) * wide] = Rs[
                    core * d.SR : (core + 1) * d.SR, pl.ds(at, wide)
                ]

    def block(i, half):
        return Gb[i, :, half].reshape(d.BLK, d.CH)

    near_first = [0]
    for k in range(1, H):
        near_first += [k, -k]
    near_first += [H]
    groups = near_first[: NZ // 2], near_first[NZ // 2 :]
    swaps, sends, takes = (
        (swap_l.at[0], swap_l.at[1], swap_r),
        (send_l.at[0], send_l.at[1], send_r),
        (recv_l0, recv_l1, recv_r),
    )
    backs = (
        (send_dl.at[0], recv_dl.at[0]),
        (send_dl.at[1], recv_dl.at[1]),
        (send_dr, recv_dr),
    )
    span = d.BLK // 2

    def swap_gram(m):
        return remote(swaps[m], sends[m].at[:, c], sw_ss.at[1 + m], sw_rs.at[1 + m], rep=sibling)

    def put_gram(m):
        width = d.PC if m == 2 else wide
        for core, mine in ((1 - c, False), (c, True)):
            value = g_s[1, core] if m == 2 else g_s[0, core, :, m * span : (m + 1) * span]
            for piece in range(NF):
                rg, cg = piece // d.CG, piece % d.CG
                part = value[rg * d.PR : (rg + 1) * d.PR, cg * width : (cg + 1) * width]
                if mine:
                    sends[m][piece, c] = part
                else:
                    swaps[m][piece] = part
            if not mine:
                swap_gram(m).start()

    def near(group, i, half, *cols):
        return jnp.concatenate([Gb[i, zat(k), half, :, *cols] for k in groups[group]], axis=0)

    def gram_left(group):
        value = 0.0
        for i in range(2):
            for h in range(2):
                value = value + lax.dot_general(
                    Gb[i, z, h],
                    near(group, i, h),
                    (((1,), (1,)), ((), ())),
                    preferred_element_type=F32,
                )
        value = ((1.0 - gram_decay) * value).astype(BF16)
        g_s[0, :, :, group * span : (group + 1) * span] = value.reshape(2, d.SR, span)
        put_gram(group)

    def gram_right(group):
        at = z * wide
        half, rest = lax.div(at, d.HC), lax.rem(at, d.HC)
        chain, off = lax.div(rest, d.CH), lax.rem(rest, d.CH)
        cols = near(group, chain, half, pl.ds(pl.multiple_of(off, wide), wide))
        for i in range(2):
            for h in range(2):
                both = lax.dot_general(
                    cols, near(group, i, h), (((0,), (0,)), ((), ())), preferred_element_type=F32
                )
                first = h * d.HC + i * d.CH
                if group == 0:
                    right_sum[:, first : first + d.CH] = both
                else:
                    both = both + right_sum[:, first : first + d.CH]
                    both = ((1.0 - gram_decay) * both).astype(BF16)
                    g_s[1, :, :, first : first + d.CH] = both.reshape(2, d.SR, d.CH)
        if group == 1:
            put_gram(2)

    def left_times(i):
        for h in range(2):
            first = h * d.HC + i * d.CH
            value = jnp.dot(Lp[...], block(i, h), preferred_element_type=F32).astype(BF16)
            for t in range(d.CH // wide):
                T_s[first // wide + t] = value[:, t * wide : (t + 1) * wide]

    def spread(m):
        swap_gram(m).wait_recv()
        aa_start(2 + m, sends[m], takes[m])

    def give_back(m):
        aa_wait(2 + m, sends[m], takes[m])
        send, recv = backs[m]

        def go(o, carry):
            for s in range(d.SLOTS):
                where = jnp.maximum(tab[blocks, o * d.SLOTS + s], 0)
                send[o * d.SLOTS + s] = takes[m][lax.div(where, 2), lax.rem(where, 2)]
            return carry

        lax.fori_loop(0, NF, go, 0)
        aa_start(5 + m, send, recv)

    def add_grams(m):
        send, recv = backs[m]
        aa_wait(5 + m, send, recv)
        side = m // 2
        if m != 1:
            for s in range(d.SLOTS):
                old_copy(side, s).wait()

        def go(s, carry):
            live = tab[blocks, f * d.SLOTS + s] >= 0
            for piece in range(NF):
                rg, cg = piece // d.CG, piece % d.CG
                rows = pl.ds(rg * d.PR, d.PR)
                if m == 2:
                    cols = pl.ds(cg * d.PC, d.PC)
                else:
                    cols = pl.ds(pl.multiple_of(zat(groups[m][cg]) * wide, wide), wide)
                added = jnp.where(live, recv[piece * d.SLOTS + s].astype(F32), 0.0)
                (new_left, new_right)[side][s, rows, cols] = (
                    gram_decay * olds[side, s, rows, cols] + added
                )
            return carry

        lax.fori_loop(0, d.SLOTS, go, 0)

    homes = (
        remote(Db.at[c, 1 - q], dir_out.at[q, c], ex_ss.at[2], ex_rs.at[2], fsdp=partner),
        remote(Db.at[1 - c, q], dir_out.at[q, c], ex_ss.at[3], ex_rs.at[3], rep=sibling),
        remote(
            Db.at[1 - c, 1 - q], dir_out.at[q, c], ex_ss.at[4], ex_rs.at[4], rep=sibling, fsdp=partner
        ),
    )

    def add_slab(dist):
        k = zat(dist)
        root = Rb[k].reshape(wide, (H + 1) * wide)
        direct = jnp.dot(T_s[k], root, preferred_element_type=F32)
        for t in range(H + 1):
            D_s[zat(dist + t)] += direct[:, t * wide : (t + 1) * wide]
        turned = jnp.concatenate([T_s[zat(dist + t)] for t in range(1, H)], axis=1)
        D_s[k] += lax.dot_general(
            turned, root[:, wide : H * wide], (((1,), (1,)), ((), ())), preferred_element_type=F32
        )

    def directions():
        for k in range(NZ):
            value = D_s[k].astype(BF16).reshape(2, d.SR, wide)
            half, at = divmod(k * wide, d.HC)
            Db[:, half, :, at : at + wide] = value
        for copy in homes:
            copy.start()
        dir_out[q, c] = Db[c, q]

    def fetch_old(s):
        for m in range(2):
            old_copy(m, s).start()

    for k in order[:3]:
        sib_copy(0, k).start()
    rs_step(0, 0)
    for k in order[3:]:
        sib_copy(0, k).start()
    rs_step(0, 1)
    for k in order:
        sib_copy(1, k).start()
    rs_step(1, 0)
    cast_root(1)
    aa_start(1, send_a.at[1], recv_a1)
    rs_step(0, 2, 3)
    cast_root(0)
    aa_start(0, send_a.at[0], recv_a0)
    rs_step(1, 1)
    tables()
    D_s[...] = jnp.zeros_like(D_s)
    rs_step(0, 4, 5)
    rs_step(1, 2)
    rs_step(0, 6)
    rs_step(1, 3)
    tab_copy.wait()
    pick_root(1)
    rs_step(1, 4)
    rs_last(0)
    rs_step(1, 5)
    pass_root(1)
    rs_step(1, 6)
    ex_g(0).wait_recv()
    ag_own(0)
    rs_last(1)
    ag_step(0, 0)
    ex_g(1).wait_recv()
    ag_own(1)
    ag_step(0, 1)
    ag_step(0, 2)
    ag_step(1, 0)
    pick_root(0)
    ag_step(0, 3)
    ag_step(1, 1)
    fetch_old(0)
    pass_root(0)
    ag_step(0, 4)
    ag_step(1, 2)
    fetch_old(1)
    ag_step(0, 5)
    ag_step(1, 3)
    fetch_old(2)
    gram_left(0)
    ag_step(0, 6)
    ag_step(1, 4)
    fetch_old(3)
    spread(0)
    gram_right(0)
    join_root(1)
    ag_own(2)
    give_back(0)
    ag_step(1, 5, 6)
    gram_right(1)
    gram_left(1)
    ag_step(2, 0)
    spread(2)
    spread(1)
    ag_step(2, 1)
    join_root(0)
    ag_step(2, 2)
    give_back(2)
    ag_step(2, 3)
    give_back(1)
    ag_step(2, 4)
    left_times(0)
    left_times(1)
    add_slab(0)
    for dist in range(1, min(3, H)):
        add_slab(-dist)
        add_slab(dist)

    for i in range(2):
        remote(sib.at[i], sib.at[i], sib_ss.at[i], sib_rs.at[i, 0], rep=sibling).wait_send()
        for stream in range(2):
            sent = rs_send.at[i, stream]
            remote(sent, sent, rs_ss.at[i, stream], rs_rs.at[i, stream, 0], rep=up).wait_send()
        ex_g(i).wait_send()
        ag_done(i)
    for m in range(2):
        aa_done(m, send_a.at[m], recv_a[m])
        aa_done(8 + m, send_b.at[m], recv_b.at[m])
        swap_root(m).wait_send()
    for m in range(3):
        swap_gram(m).wait_send()
        aa_done(2 + m, sends[m], takes[m])
    aa_done(5, *backs[0])
    add_grams(0)

    ag_step(2, 5)
    for dist in range(3, H):
        add_slab(-dist)
        add_slab(dist)
    ag_step(2, 6)
    add_slab(H)
    directions()
    add_grams(2)
    add_grams(1)
    ag_done(2)
    for m in range(1, 3):
        aa_done(5 + m, *backs[m])
    for copy in homes:
        copy.wait()


def local(gradients, old_left, old_right, left_root, right_root, owner_plan):
    rep, fsdp = lax.axis_size("rep"), lax.axis_size("fsdp")
    _, layers, rows, home = gradients.shape
    slots = old_left.shape[0]
    d = Dims(rep, fsdp, layers, rows, home, slots)

    S, NZ, NF = d.STEPS, d.NZ, d.NF
    CR = 2 * d.SR
    piece = (d.PR, d.PC)
    vmem = lambda *shape: pltpu.VMEM(shape, BF16)
    wide = lambda *shape: pltpu.VMEM(shape, F32)
    dma = lambda *shape: pltpu.SemaphoreType.DMA(shape)
    whole = pl.BlockSpec(memory_space=pltpu.VMEM)
    away = pl.BlockSpec(memory_space=pl.ANY)
    new_left, new_right, direction = pl.pallas_call(
        functools.partial(kernel, d),
        out_shape=(
            jax.ShapeDtypeStruct(old_left.shape, F32),
            jax.ShapeDtypeStruct(old_right.shape, F32),
            jax.ShapeDtypeStruct((2, 2, d.SR, d.HC), BF16),
        ),
        in_specs=[away] * 6,
        out_specs=(whole,) * 3,
        scratch_shapes=[
            pltpu.SMEM(owner_plan.shape, jnp.int32),
            pltpu.VMEM((owner_plan.size + 8, 128), jnp.int32),
            pltpu.SMEM((owner_plan.size + 8, 128), jnp.int32),
            vmem(NZ, 2, CR, d.HC),
            vmem(2, NZ, 2, CR, d.CH),
            vmem(2, 2, S, CR, d.CH),
            vmem(2, 2, S, CR, d.CH),
            vmem(2, 2, CR, d.CH),
            wide(2, slots, d.SR, d.BLK),
            wide(2, slots, d.SR, d.BLK),
            vmem(2, NF * slots, *piece),
            vmem(NF * slots, *piece),
            vmem(NF * slots, *piece),
            vmem(2, NF, *piece),
            vmem(2, NF, 2, *piece),
            vmem(2, NF, 2, *piece),
            vmem(CR, d.BLK),
            vmem(CR, d.BLK),
            vmem(2, NZ, 2, CR, d.CH),
            vmem(NZ, 2, d.SR, (d.H + 1) * CR),
            vmem(2, 2, d.SR, d.BLK),
            wide(CR, d.BLK),
            vmem(NZ, CR, CR),
            wide(NZ, CR, CR),
            vmem(NF, *piece),
            vmem(NF, 2, *piece),
            vmem(NF, 2, *piece),
            vmem(2, NF, d.PR, CR),
            vmem(2, NF, 2, d.PR, CR),
            vmem(NF, 2, d.PR, CR),
            vmem(NF, 2, d.PR, CR),
            vmem(NF * slots, *piece),
            vmem(NF * slots, *piece),
            vmem(2, NF * slots, d.PR, CR),
            vmem(2, NF * slots, d.PR, CR),
            vmem(2, 2, d.SR, d.HC),
            dma(NZ),
            dma(2),
            dma(2, slots),
            pltpu.SemaphoreType.DMA,
            pltpu.SemaphoreType.DMA,
            dma(2),
            dma(2, NZ),
            dma(2, 2),
            dma(2, 2, S),
            dma(10),
            dma(10),
            dma(6),
            dma(6),
            dma(5),
            dma(5),
            dma(3),
            dma(3, 2, S),
        ],
        compiler_params=pltpu.CompilerParams(
            collective_id=0, has_side_effects=True, vmem_limit_bytes=51 * 1024 * 1024
        ),
        cost_estimate=pl.CostEstimate(
            flops=2 * 5 * 2 * d.SR * d.BLK * d.BLK,
            bytes_accessed=2 * gradients.size + 24 * left_root.size,
            transcendentals=0,
        ),
    )(
        gradients.reshape(2, 2, NZ, CR, home),
        old_left,
        old_right,
        left_root,
        right_root,
        owner_plan,
    )
    return new_left, new_right, direction.reshape(layers, d.SR, home)


def solution(mesh):
    return jax.shard_map(
        local,
        mesh=mesh,
        in_specs=(
            P("rep", None, None, "fsdp"),
            P("fsdp", "rep", None),
            P("fsdp", "rep", None),
            P("fsdp", "rep", None),
            P("fsdp", "rep", None),
            P(),
        ),
        out_specs=(P("fsdp", "rep", None), P("fsdp", "rep", None), P(None, "rep", "fsdp")),
        check_vma=False,
    )
```
